128 devices in a mesh: dp: 16 (over x, y), row: 2 (over z_lo), col: 4 (over z_hi, core).
Axes of the slice: x: 4, y: 4, z: 4 (z_hi: 2, z_lo: 2; z = z_hi * 2 + z_lo), core: 2. Of those that a mesh axis runs over, the one named last changes fastest.
Arguments:
- tokens: bfloat16 [16384, 1152], P(('dp', 'col'), 'row'), may hold values from -6 to 6
- doc_lengths: int32 [16, 6], P('dp'), may hold values from 0 to 1024, as said below
- w_query: bfloat16 [1152, 1024], P('row', 'col'), may hold values from -0.1875 to 0.1875
- w_key: bfloat16 [1152, 256], P('row', 'col'), may hold values from -0.1875 to 0.1875
- w_value: bfloat16 [1152, 256], P('row', 'col'), may hold values from -0.1875 to 0.1875
- w_out: bfloat16 [1024, 1152], P('col', 'row'), may hold values from -0.1875 to 0.1875
- w_gate: bfloat16 [1152, 6912], P('row', 'col'), may hold values from -0.1875 to 0.1875
- w_up: bfloat16 [1152, 6912], P('row', 'col'), may hold values from -0.1875 to 0.1875
- w_down: bfloat16 [6912, 1152], P('col', 'row'), may hold values from -0.078125 to 0.078125
- gain_attn_in: float32 [1152], P('row'), may hold values from 0.25 to 1.75
- gain_attn_out: float32 [1152], P('row'), may hold values from 0.25 to 1.75
- gain_ff_in: float32 [1152], P('row'), may hold values from 0.25 to 1.75
- gain_ff_out: float32 [1152], P('row'), may hold values from 0.25 to 1.75
- gain_query: float32 [256], replicated, may hold values from 0.25 to 1.75
- gain_key: float32 [256], replicated, may hold values from 0.25 to 1.75
- cotangent: bfloat16 [16384, 1152], P(('dp', 'col'), 'row'), may hold values from -6 to 6
Outputs:
- mixed: bfloat16 [16384, 1152], P(('dp', 'col'), 'row')
- grad_tokens: float32 [16384, 1152], P(('dp', 'col'), 'row')
- grad_w_query: float32 [1152, 1024], P('row', 'col')
- grad_w_key: float32 [1152, 256], P('row', 'col')
- grad_w_value: float32 [1152, 256], P('row', 'col')
- grad_w_out: float32 [1024, 1152], P('col', 'row')
- grad_w_gate: float32 [1152, 6912], P('row', 'col')
- grad_w_up: float32 [1152, 6912], P('row', 'col')
- grad_w_down: float32 [6912, 1152], P('col', 'row')
- grad_gain_attn_in: float32 [1152], P('row')
- grad_gain_attn_out: float32 [1152], P('row')
- grad_gain_ff_in: float32 [1152], P('row')
- grad_gain_ff_out: float32 [1152], P('row')
- grad_gain_query: float32 [256], replicated
- grad_gain_key: float32 [256], replicated
The draws below stay inside these ranges and needn't reach their ends.
Inputs may be any that keep to these rules, and one draw needn't show every extreme that they name: `doc_lengths`: row g lists the lengths of data group g's sequences in the order in which they lie in its 1024 slots; zeros are empty entries. Each row sums to at most 1024; in every draw one row is a single sequence of exactly 1024. In every row one sequence begins in the first 256 slots and ends in the last 256.
All inputs are finite; a program needn't handle non-finite values.
Results may differ from the reference program's by a relative error of at most 0.025.
Values may be sent and summed in bfloat16 or wider, within the bound.
No kernel may reach another device: no remote copies, remote signals or barrier semaphores. Data moves between devices by JAX's collectives and lax.ppermute only.
A program may use at most 128 MiB of HBM per device.

```python
from functools import partial
import jax
import jax.numpy as jnp
from jax import lax

D = 1152
H = 4
HD = 256
FF = 6912
WINDOW = 512
SLOTS = 6
CAP = 1024
TOKENS = 16384
N_DP = 16


def draw_doc_lengths(key, part):
    key = jax.random.fold_in(key, 11)
    capacity = CAP
    quarter = capacity // 4
    subkeys = jax.random.split(key, 5)
    leading = jax.random.randint(subkeys[0], (N_DP,), 0, quarter)
    lowest = jnp.maximum(capacity - quarter + 1 - leading, capacity // 2 + 1)
    longest = jax.random.randint(subkeys[1], (N_DP,), lowest, capacity - leading + 1)
    chosen = jax.random.randint(subkeys[2], (), 0, N_DP)
    groups = jnp.arange(N_DP, dtype=jnp.int32)
    leading = jnp.where(groups == chosen, 0, leading)
    longest = jnp.where(groups == chosen, capacity, longest)
    remaining = capacity - leading - longest
    used = jax.random.randint(subkeys[3], (N_DP,), 0, remaining + 1)
    cuts = jax.random.randint(subkeys[4], (N_DP, SLOTS - 3), 0, used[:, None] + 1)
    cuts = jnp.sort(cuts, axis=1)
    edges = jnp.concatenate([jnp.zeros((N_DP, 1), jnp.int32), cuts.astype(jnp.int32), used[:, None].astype(jnp.int32)], axis=1)
    pieces = edges[:, 1:] - edges[:, :-1]
    return jnp.concatenate([leading[:, None], longest[:, None], pieces], axis=1).astype(jnp.int32)


def level_of(key, extent, cuts, smallest, largest):
    loudness = 1.0
    for axis_at, blocks in cuts:
        heights = jax.random.uniform(jax.random.fold_in(jax.random.fold_in(key, 6), axis_at), (blocks,), jnp.float32, smallest / len(cuts), largest / len(cuts))
        loudness = loudness * jnp.repeat(jnp.exp(heights), extent[axis_at] // blocks).reshape((-1,) + (1,) * (len(extent) - 1 - axis_at))
    return loudness


def noise(own_key, shape, scale, bound, shards=(), held_as=jnp.bfloat16):
    factor_of = level_of(own_key, shape, shards, -0.22, 0.18) if shards else 1.0
    array = jax.random.normal(own_key, shape, jnp.float32) * scale * factor_of
    return jnp.minimum(jnp.maximum(array, -bound), bound).astype(held_as)


def setup_inputs(seed: int = 0) -> dict:
    streams_of = jax.random.split(jax.random.key(seed), 17)
    return {
        "tokens": noise(streams_of[0], (TOKENS, D), 1.0, 6.0, ((0, 64), (1, 2))),
        "doc_lengths": draw_doc_lengths(jax.random.fold_in(streams_of[16], 71), 0),
        "w_query": noise(streams_of[2], (D, H * HD), D ** -0.5, 0.1875, ((0, 2), (1, 4))),
        "w_key": noise(streams_of[3], (D, HD), D ** -0.5, 0.1875, ((0, 2), (1, 4))),
        "w_value": noise(streams_of[4], (D, HD), D ** -0.5, 0.1875, ((0, 2), (1, 4))),
        "w_out": noise(streams_of[5], (H * HD, D), (H * HD) ** -0.5, 0.1875, ((0, 4), (1, 2))),
        "w_gate": noise(streams_of[6], (D, FF), D ** -0.5, 0.1875, ((0, 2), (1, 4))),
        "w_up": noise(streams_of[7], (D, FF), D ** -0.5, 0.1875, ((0, 2), (1, 4))),
        "w_down": noise(streams_of[8], (FF, D), FF ** -0.5, 0.078125, ((0, 4), (1, 2))),
        "gain_attn_in": jnp.clip(1.0 + 0.15 * jax.random.normal(streams_of[9], (D,), jnp.float32), 0.25, 1.75),
        "gain_attn_out": jnp.clip(1.0 + 0.15 * jax.random.normal(streams_of[10], (D,), jnp.float32), 0.25, 1.75),
        "gain_ff_in": jnp.clip(1.0 + 0.15 * jax.random.normal(streams_of[11], (D,), jnp.float32), 0.25, 1.75),
        "gain_ff_out": jnp.clip(1.0 + 0.15 * jax.random.normal(streams_of[12], (D,), jnp.float32), 0.25, 1.75),
        "gain_query": jnp.clip(1.0 + 0.15 * jax.random.normal(streams_of[13], (HD,), jnp.float32), 0.25, 1.75),
        "gain_key": jnp.clip(1.0 + 0.15 * jax.random.normal(streams_of[14], (HD,), jnp.float32), 0.25, 1.75),
        "cotangent": noise(streams_of[15], (TOKENS, D), 1.0, 6.0, ((0, 64), (1, 2))),
    }


@jax.custom_vjp
def low(v):
    return lax.optimization_barrier(v.astype(jnp.bfloat16)).astype(jnp.float32)

@jax.custom_vjp
def low_back(v):
    return v

def low_keep(v):
    return (low(v), None)

def low_pass(kept, grad):
    return (grad,)

def back_keep(v):
    return (v, None)

def back_low(kept, grad):
    return (low(grad),)
low.defvjp(low_keep, low_pass)
low_back.defvjp(back_keep, back_low)
EPSILON = 1e-06
ROPE_BASE = 10000.0
MASKED = -1e+30

def layout(lengths_row, capacity):
    slot_count = lengths_row.shape[0]
    seq_ends = jnp.cumsum(lengths_row).astype(jnp.int32)
    places = jnp.arange(capacity, dtype=jnp.int32)
    sequence = lax.optimization_barrier(jnp.sum((places[:, None] >= seq_ends[None, :]).astype(jnp.int32), axis=1)).astype(jnp.int32)
    starts = jnp.concatenate([jnp.zeros((1,), jnp.int32), seq_ends])
    labels = jnp.arange(slot_count + 1, dtype=jnp.int32)
    start_of = lax.optimization_barrier(jnp.sum(jnp.where(sequence[:, None] == labels[None, :], starts[None, :], 0), axis=1)).astype(jnp.int32)
    live_rows = (places < seq_ends[slot_count - 1]).astype(jnp.int32)
    return (sequence, places - start_of, live_rows)

def matmul(left, right):
    return jnp.dot(left, right, precision=lax.Precision.HIGHEST)

def norm_rows(values, gain_vector):
    return values * lax.rsqrt(lax.optimization_barrier(jnp.mean(values * values, axis=-1, keepdims=True)) + EPSILON) * gain_vector

def rotate(values, positions):
    full_width = values.shape[-1]
    half_width = full_width // 2
    frequency = ROPE_BASE ** (-2.0 * jnp.arange(half_width, dtype=jnp.float32) / full_width)
    angles = positions.astype(jnp.float32).reshape((-1,) + (1,) * (values.ndim - 1)) * frequency
    cosine = jnp.cos(angles)
    sine_part = jnp.sin(angles)
    first_half = values[..., :half_width]
    second_half = values[..., half_width:]
    return jnp.concatenate([first_half * cosine - second_half * sine_part, second_half * cosine + first_half * sine_part], axis=-1)

def group_attention(queries, keys_turned, values_low, sequence, positions):
    capacity = queries.shape[0]
    block_rows = capacity if capacity % 512 != 0 else 512
    score_scale = queries.shape[-1] ** (-0.5)

    def one_block(first_row):
        query_part = lax.dynamic_slice_in_dim(queries, first_row, block_rows, 0)
        row_seq = lax.dynamic_slice_in_dim(sequence, first_row, block_rows, 0)
        row_pos = lax.dynamic_slice_in_dim(positions, first_row, block_rows, 0)
        distance = row_pos[:, None] - positions[None, :]
        allowed = (row_seq[:, None] == sequence[None, :]) & (distance >= 0) & (distance < WINDOW)
        raw_scores = low_back(jnp.einsum('qhd,kd->hqk', query_part, keys_turned, precision=lax.Precision.HIGHEST))
        scores = jnp.where(allowed[None], raw_scores * score_scale, MASKED)
        highest = lax.optimization_barrier(jnp.max(scores, axis=2, keepdims=True))
        weights = jnp.exp(scores - highest)
        shares = low(weights / lax.optimization_barrier(jnp.sum(weights, axis=2, keepdims=True)))
        return low_back(low(jnp.einsum('hqk,kd->qhd', shares, values_low, precision=lax.Precision.HIGHEST)))
    starts = jnp.arange(capacity // block_rows, dtype=jnp.int32) * block_rows
    return lax.map(jax.checkpoint(one_block), starts).reshape(queries.shape)

def group_step(group_parts):
    return group_attention(group_parts[0], group_parts[1], group_parts[2], group_parts[3], group_parts[4])

def block_forward(tokens, w_query, w_key, w_value, w_out, w_gate, w_up, w_down, gain_attn_in, gain_attn_out, gain_ff_in, gain_ff_out, gain_query, gain_key, sequence, positions):
    normed_in = low(norm_rows(tokens, gain_attn_in))
    pre_query = low_back(matmul(normed_in, w_query)).reshape(-1, H, HD)
    pre_key = low(low_back(matmul(normed_in, w_key)))
    pre_value = low(low_back(matmul(normed_in, w_value)))
    queries = low(rotate(norm_rows(pre_query, gain_query), positions))
    keys_turned = low(rotate(norm_rows(pre_key, gain_key), positions))
    attended = lax.map(group_step, (queries.reshape(N_DP, CAP, H, HD), keys_turned.reshape(N_DP, CAP, HD), pre_value.reshape(N_DP, CAP, HD), sequence.reshape(N_DP, CAP), positions.reshape(N_DP, CAP)))
    attended = attended.reshape(TOKENS, H * HD)
    branch_attn = low_back(matmul(attended, w_out))
    hidden_mid = tokens + norm_rows(branch_attn, gain_attn_out)
    normed_ff = low(norm_rows(hidden_mid, gain_ff_in))
    gate = low_back(matmul(normed_ff, w_gate))
    upward = low_back(matmul(normed_ff, w_up))
    activated = low(jax.nn.gelu(gate, approximate=True) * upward)
    branch_ff = low_back(matmul(activated, w_down))
    return hidden_mid + norm_rows(branch_ff, gain_ff_out)

def reference(tokens, doc_lengths, w_query, w_key, w_value, w_out, w_gate, w_up, w_down, gain_attn_in, gain_attn_out, gain_ff_in, gain_ff_out, gain_query, gain_key, cotangent):
    sequence, positions, live_rows = jax.vmap(partial(layout, capacity=CAP))(doc_lengths)
    sequence = sequence.reshape(TOKENS)
    positions = positions.reshape(TOKENS)
    live_rows = live_rows.reshape(TOKENS)
    floats = tuple((argument.astype(jnp.float32) for argument in (tokens, w_query, w_key, w_value, w_out, w_gate, w_up, w_down, gain_attn_in, gain_attn_out, gain_ff_in, gain_ff_out, gain_query, gain_key)))
    result, pullback = jax.vjp(partial(block_forward, sequence=sequence, positions=positions), *floats)
    gradients = pullback(cotangent.astype(jnp.float32) * live_rows.astype(jnp.float32)[:, None])
    return (result.astype(jnp.bfloat16), gradients[0], gradients[1], gradients[2], gradients[3], gradients[4], gradients[5], gradients[6], gradients[7], gradients[8], gradients[9], gradients[10], gradients[11], gradients[12], gradients[13])
```

```python
import jax
import jax.numpy as jnp
from jax import lax
from jax.sharding import PartitionSpec as P

WINDOW = 512
EPSILON = 1e-06
ROPE_BASE = 10000.0
MASKED = -1e30
GROUP = ("row", "col")
BF = jnp.bfloat16
F32 = jnp.float32
OWN = 128
D = 1152
HALF = 576
HIDDEN = 864
ROW_PART = 36
BLOCKS = ((0, 0), (0, 1), (2, 0), (2, 1), (1, 0), (1, 1), (3, 0), (3, 1))


def member(z, core):
    return (z % 2) * 4 + (z // 2) * 2 + core


def z_pairs(step):
    return [(member(z, c), member((z + step) % 4, c)) for z in range(4) for c in range(2)]


CORE_PAIRS = [(member(z, c), member(z, 1 - c)) for z in range(4) for c in range(2)]
ROW_PAIRS = [(0, 1), (1, 0)]


def move_z(values, step):
    return lax.ppermute(values, GROUP, z_pairs(step % 4))


def move_core(values):
    return lax.ppermute(values, GROUP, CORE_PAIRS)


def move_row(values):
    return lax.ppermute(values, "row", ROW_PAIRS)


def move_plane(values, axis, step):
    if axis == "x":
        pairs = [(x * 4 + y, ((x + step) % 4) * 4 + y) for x in range(4) for y in range(4)]
    else:
        pairs = [(x * 4 + y, x * 4 + (y + step) % 4) for x in range(4) for y in range(4)]
    return lax.ppermute(values, "dp", pairs)


def gather_blocks(own, steps):
    held = {0: own}
    for step in steps:
        held[step] = move_z(own, step)
    order = [0] + [s for s in (2, 1, 3) if s in steps]
    swapped = {0: move_core(own)}
    for step in (s for s in (1, 3, 2) if s in steps):
        swapped[step] = move_core(held[step])
    pieces = []
    for step in order:
        pieces += [held[step], swapped[step]]
    return jnp.concatenate(pieces, axis=0)


def reduce_blocks(partial, steps):
    order = [0] + [s for s in (2, 1, 3) if s in steps]
    rows = partial.shape[0] // (2 * len(order))
    blocks = partial.reshape(len(order), 2, rows, partial.shape[1])
    total = None
    arrived = []
    for at in reversed(range(len(order))):
        swapped = move_core(blocks[at, 1].astype(BF)).astype(F32)
        both = blocks[at, 0].astype(F32) + swapped
        if at == 0:
            total = both
        else:
            arrived.append(move_z(both.astype(BF), -order[at]))
    for piece in arrived:
        total = total + piece.astype(F32)
    return total


def reduce_ring(parts, coordinate, axis):
    total = lax.dynamic_index_in_dim(parts, coordinate, 0, keepdims=False).astype(F32)
    for step in (1, 3, 2):
        sent = lax.dynamic_index_in_dim(parts, (coordinate + step) % 4, 0, keepdims=False)
        total = total + move_plane(sent, axis, step).astype(F32)
    return total.astype(BF)


def gather_ring(part, coordinate, axis):
    result = jnp.zeros((4,) + part.shape, part.dtype)
    result = lax.dynamic_update_index_in_dim(result, part, coordinate, 0)
    for step in (1, 3, 2):
        got = move_plane(part, axis, step)
        result = lax.dynamic_update_index_in_dim(result, got, (coordinate + 4 - step) % 4, 0)
    return result


def reduce_plane(values, at, first, second):
    rows, width = values.shape
    once = reduce_ring(values.reshape(4, rows // 4, width), at[first], first)
    return reduce_ring(once.reshape(4, rows // 16, width), at[second], second)


def gather_plane(part, at, first, second):
    rows, width = part.shape
    once = gather_ring(part, at[second], second).reshape(4 * rows, width)
    return gather_ring(once, at[first], first).reshape(16 * rows, width)


def layout(lengths_row, places):
    slot_count = lengths_row.shape[0]
    seq_ends = jnp.cumsum(lengths_row)
    sequence = jnp.sum((places[:, None] >= seq_ends[None, :]).astype(jnp.int32), axis=1)
    starts = jnp.concatenate([jnp.zeros((1,), jnp.int32), seq_ends])
    labels = jnp.arange(slot_count + 1, dtype=jnp.int32)
    start_of = jnp.sum(jnp.where(sequence[:, None] == labels[None, :], starts[None, :], 0), axis=1)
    live_rows = (places < seq_ends[slot_count - 1]).astype(jnp.int32)
    return (sequence, places - start_of, live_rows)


def rotation(positions, full_width):
    half_width = full_width // 2
    frequency = ROPE_BASE ** (-2.0 * jnp.arange(half_width, dtype=F32) / full_width)
    angles = positions.astype(F32)[:, None] * frequency
    return (jnp.cos(angles), jnp.sin(angles))


def rotate(values, cosine, sine):
    half_width = values.shape[1] // 2
    first, second = values[:, :half_width], values[:, half_width:]
    return jnp.concatenate(
        [first * cosine - second * sine, second * cosine + first * sine], axis=1
    )


def inverse_of(values):
    return lax.rsqrt(jnp.mean(values * values, axis=1, keepdims=True) + EPSILON)


def norm_back(values, inverse, gain, incoming):
    inner = jnp.mean(incoming * gain * values, axis=1, keepdims=True)
    return inverse * gain * incoming - values * (inverse * inverse * inverse * inner)


def dot(left, right, left_dim=1, right_dim=0):
    return lax.dot_general(
        left, right, (((left_dim,), (right_dim,)), ((), ())), preferred_element_type=F32
    )


def body(
    tokens,
    doc_lengths,
    w_query,
    w_key,
    w_value,
    w_out,
    w_gate,
    w_up,
    w_down,
    gain_attn_in,
    gain_attn_out,
    gain_ff_in,
    gain_ff_out,
    gain_query,
    gain_key,
    cotangent,
):
    row = lax.axis_index("row")
    col = lax.axis_index("col")
    plane = lax.axis_index("dp")
    at = {"x": plane // 4, "y": plane % 4}
    z, core = (col // 2) * 2 + row, col % 2
    head_dim = gain_query.shape[0]
    score_scale = head_dim ** (-0.5)

    def in_order(own, other, axis):
        return jnp.where(
            row == 0,
            jnp.concatenate([own, other], axis=axis),
            jnp.concatenate([other, own], axis=axis),
        )

    def whole_rows(block):
        halves = block.reshape(2, OWN, HALF)
        other = move_row(lax.dynamic_index_in_dim(halves, 1 - row, 0, keepdims=False))
        return in_order(lax.dynamic_index_in_dim(halves, row, 0, keepdims=False), other, 1)

    def split_rows(owned, sent):
        halves = owned.reshape(OWN, 2, HALF)
        sent_halves = sent.reshape(OWN, 2, HALF)
        other = move_row(lax.dynamic_index_in_dim(sent_halves, 1 - row, 1, keepdims=False))
        own = lax.dynamic_index_in_dim(halves, row, 1, keepdims=False)
        return in_order(own, other.astype(own.dtype), 0)

    def half_of(vector):
        return lax.dynamic_slice_in_dim(vector, row * HALF, HALF, 0)

    residual = whole_rows(tokens).astype(F32)
    gain_pack = jnp.stack([gain_attn_in, gain_attn_out, gain_ff_in, gain_ff_out], 0)
    gain_all = in_order(gain_pack, move_row(gain_pack), 1)
    full_attn_in, full_attn_out, full_ff_in, full_ff_out = (gain_all[i : i + 1] for i in range(4))

    inverse_in = inverse_of(residual)
    normed_own = (residual * inverse_in * full_attn_in).astype(BF)
    normed_in = gather_blocks(normed_own, (1, 3, 2))

    query_weights = in_order(w_query, move_row(w_query), 0)
    kv_own = jnp.concatenate([w_key, w_value], axis=1)
    kv_blocks = gather_blocks(kv_own[None], (1, 3, 2))
    owner_row = jnp.stack([((z - k) % 4) % 2 for k, d in BLOCKS])
    owner_col = jnp.stack([((z - k + 4) % 4) // 2 * 2 + (core + d) % 2 for k, d in BLOCKS])
    owner = owner_row * 4 + owner_col
    place_of = jnp.sum(
        jnp.where(owner[None, :] == jnp.arange(8)[:, None], jnp.arange(8)[None, :], 0), axis=1
    )
    kv_weights = (
        jnp.take(kv_blocks, place_of, axis=0)
        .reshape(2, 4, HALF, 2, 64)
        .transpose(0, 2, 3, 1, 4)
        .reshape(D, 512)
    )
    out_weights = in_order(w_out, move_row(w_out), 1)

    stacked = jnp.stack([w_gate, w_up, w_down.T], axis=0)
    piece = lax.dynamic_slice(
        stacked, (0, plane * ROW_PART, (1 - row) * HIDDEN), (3, ROW_PART, HIDDEN)
    )
    gathered = lax.all_gather(move_row(piece), "dp", axis=0, tiled=False)
    other_half = gathered.transpose(1, 0, 2, 3).reshape(3, HALF, HIDDEN)
    own_half = lax.dynamic_slice_in_dim(stacked, row * HIDDEN, HIDDEN, 2)
    ff_weights = in_order(own_half, other_half, 1)
    gate_weights, up_weights, down_weights = ff_weights[0], ff_weights[1], ff_weights[2]

    starts = owner_col * 256 + owner_row * OWN
    places = (starts[:, None] + jnp.arange(OWN, dtype=jnp.int32)[None, :]).reshape(-1)
    sequence, positions, live_rows = layout(doc_lengths[0], places)
    live_own = live_rows[:OWN].astype(F32)[:, None]
    cosine, sine = rotation(positions, head_dim)
    q_rows = 512
    q_cosine, q_sine = cosine[:q_rows], sine[:q_rows]
    distance = positions[:q_rows, None] - positions[None, :]
    allowed = (
        (sequence[:q_rows, None] == sequence[None, :]) & (distance >= 0) & (distance < WINDOW)
    )

    pre_query = dot(normed_in[:q_rows], query_weights)
    key_value = dot(normed_in, kv_weights).astype(BF)
    pre_key = key_value[:, :head_dim].astype(F32)
    values_low = key_value[:, head_dim:]
    inverse_q = inverse_of(pre_query)
    inverse_k = inverse_of(pre_key)
    queries_low = rotate(pre_query * inverse_q * gain_query[None], q_cosine, q_sine).astype(BF)
    keys_low = rotate(pre_key * inverse_k * gain_key[None], cosine, sine).astype(BF)
    scores = jnp.where(allowed, dot(queries_low, keys_low, 1, 1) * score_scale, MASKED)
    highest = jnp.max(scores, axis=1, keepdims=True)
    weights = jnp.exp(scores - highest)
    totals = jnp.sum(weights, axis=1, keepdims=True)
    shares = weights / totals
    shares_low = shares.astype(BF)
    attended = dot(shares_low, values_low).astype(BF)

    branch_attn = reduce_blocks(dot(attended, out_weights), (2,))
    inverse_attn_out = inverse_of(branch_attn)
    hidden_mid = residual + branch_attn * inverse_attn_out * full_attn_out
    inverse_ff_in = inverse_of(hidden_mid)
    normed_ff = gather_blocks((hidden_mid * inverse_ff_in * full_ff_in).astype(BF), (1, 3, 2))

    gate = dot(normed_ff, gate_weights)
    upward = dot(normed_ff, up_weights)
    activated, activate_back = jax.vjp(
        lambda gate_part, upward_part: jax.nn.gelu(gate_part, approximate=True) * upward_part,
        gate,
        upward,
    )
    activated_low = activated.astype(BF)
    branch_ff = reduce_blocks(dot(activated_low, down_weights, 1, 1), (1, 3, 2))
    inverse_ff_out = inverse_of(branch_ff)
    mixed_own = (hidden_mid + branch_ff * inverse_ff_out * full_ff_out).astype(BF)

    grad_result = whole_rows(cotangent).astype(F32) * live_own
    gain_sum_ff_out = jnp.sum(grad_result * branch_ff * inverse_ff_out, axis=0)
    grad_branch_ff = norm_back(branch_ff, inverse_ff_out, full_ff_out, grad_result).astype(BF)
    grad_branch_all = gather_blocks(grad_branch_ff, (1, 3, 2))
    grad_activated = dot(grad_branch_all, down_weights)
    grad_gate, grad_up = activate_back(grad_activated)
    grad_gate, grad_up = grad_gate.astype(BF), grad_up.astype(BF)
    grad_normed_ff = reduce_blocks(
        dot(grad_gate, gate_weights, 1, 1) + dot(grad_up, up_weights, 1, 1), (1, 3, 2)
    )
    part_down = dot(grad_branch_all, activated_low, 0, 0).astype(BF)
    part_gate = dot(normed_ff, grad_gate, 0, 0).astype(BF)
    part_up = dot(normed_ff, grad_up, 0, 0).astype(BF)

    grad_hidden = grad_result + norm_back(hidden_mid, inverse_ff_in, full_ff_in, grad_normed_ff)
    gain_sum_attn_out = jnp.sum(grad_hidden * branch_attn * inverse_attn_out, axis=0)
    grad_branch_attn = norm_back(
        branch_attn, inverse_attn_out, full_attn_out, grad_hidden
    ).astype(BF)
    grad_attn_all = gather_blocks(grad_branch_attn, (2,))
    grad_attended = dot(grad_attn_all, out_weights, 1, 1).astype(BF)
    part_out = dot(grad_attn_all, attended, 0, 0)

    grad_shares = dot(grad_attended, values_low, 1, 1)
    inner = jnp.sum(shares * grad_shares, axis=1, keepdims=True)
    grad_scores = (shares * (grad_shares - inner) * score_scale).astype(BF)
    grad_query = dot(grad_scores, keys_low)
    grad_key = dot(grad_scores, queries_low, 0, 0)
    grad_value = dot(shares_low, grad_attended, 0, 0)
    turned_q = rotate(grad_query, q_cosine, -q_sine)
    turned_k = rotate(grad_key, cosine, -sine)
    gain_sum_query = jnp.sum(turned_q * pre_query * inverse_q, axis=0)
    gain_sum_key = jnp.sum(turned_k * pre_key * inverse_k, axis=0)
    grad_pre_query = norm_back(pre_query, inverse_q, gain_query[None], turned_q).astype(BF)
    grad_pre_key = norm_back(pre_key, inverse_k, gain_key[None], turned_k)
    grad_kv = jnp.concatenate([grad_pre_key, grad_value], axis=1).astype(BF)

    from_kv = dot(grad_kv, kv_weights, 1, 1)
    from_query = dot(grad_pre_query, query_weights, 1, 1)
    grad_normed_in = reduce_blocks(
        jnp.concatenate([from_kv[:q_rows] + from_query, from_kv[q_rows:]], axis=0), (1, 3, 2)
    )
    grad_tokens_own = grad_hidden + norm_back(residual, inverse_in, full_attn_in, grad_normed_in)

    mixed = split_rows(mixed_own, mixed_own)
    grad_tokens = split_rows(grad_tokens_own, grad_tokens_own.astype(BF))

    parts = jnp.concatenate([part_gate, part_up, part_down], axis=1)
    halves = parts.reshape(2, HALF, 3 * HIDDEN)
    own_part = lax.dynamic_index_in_dim(halves, row, 0, keepdims=False)
    other_part = lax.dynamic_index_in_dim(halves, 1 - row, 0, keepdims=False)
    own_piece = reduce_plane(own_part, at, "x", "y")
    peer_piece = move_row(reduce_plane(other_part, at, "y", "x"))
    own_sum = gather_plane(own_piece, at, "x", "y").astype(F32)
    peer_sum = gather_plane(peer_piece, at, "y", "x").astype(F32)

    def both_blocks(i):
        cut = slice(i * HIDDEN, (i + 1) * HIDDEN)
        return in_order(own_sum[:, cut], peer_sum[:, cut], 1)

    grad_w_gate, grad_w_up, grad_w_down = both_blocks(0), both_blocks(1), both_blocks(2).T

    part_query = dot(normed_in[:q_rows], grad_pre_query, 0, 0)
    pair = jnp.concatenate([part_query, part_out], axis=1).reshape(2, HALF, 512)
    pair_own = lax.dynamic_index_in_dim(pair, row, 0, keepdims=False)
    pair_other = lax.dynamic_index_in_dim(pair, 1 - row, 0, keepdims=False).astype(BF)
    pair_sum = (pair_own + move_row(pair_other).astype(F32)).astype(BF)
    part_kv = (
        dot(normed_in, grad_kv, 0, 0)
        .reshape(2, HALF, 2, 4, 64)
        .transpose(0, 3, 1, 2, 4)
        .reshape(8, HALF, 128)
    )
    kv_sum = reduce_blocks(
        jnp.take(part_kv, owner, axis=0).reshape(8 * HALF, 128), (1, 3, 2)
    ).astype(BF)
    first = pair_sum[:, 256:]
    second = jnp.concatenate([pair_sum[:, :256], kv_sum], axis=1)
    first_sum = gather_plane(reduce_plane(first, at, "x", "y"), at, "x", "y").astype(F32)
    second_sum = gather_plane(reduce_plane(second, at, "y", "x"), at, "y", "x").astype(F32)
    grad_w_query = second_sum[:, :256]
    grad_w_key = second_sum[:, 256:320]
    grad_w_value = second_sum[:, 320:384]
    grad_w_out = first_sum.T

    def over_cols(vector):
        vector = vector + move_core(vector)
        return vector + move_z(vector, 2)

    products_ff = jnp.sum(grad_w_gate * w_gate.astype(F32), axis=1) + jnp.sum(
        grad_w_up * w_up.astype(F32), axis=1
    )
    products_in = (
        jnp.sum(grad_w_query * w_query.astype(F32), axis=1)
        + jnp.sum(grad_w_key * w_key.astype(F32), axis=1)
        + jnp.sum(grad_w_value * w_value.astype(F32), axis=1)
    )
    products = over_cols(jnp.stack([products_ff, products_in]))
    grad_gain_ff_in = products[0] / gain_ff_in
    grad_gain_attn_in = products[1] / gain_attn_in

    packed = jnp.concatenate(
        [gain_sum_ff_out, gain_sum_attn_out, gain_sum_query, gain_sum_key]
    ).reshape(22, 128)
    for axis in ("x", "y"):
        packed = (packed + move_plane(packed, axis, 2)) + (
            move_plane(packed, axis, 1) + move_plane(packed, axis, 3)
        )
    packed = packed + move_core(packed)
    packed = (packed + move_z(packed, 2)) + (move_z(packed, 1) + move_z(packed, 3))
    packed = packed.reshape(-1)
    return (
        mixed,
        grad_tokens,
        grad_w_query,
        grad_w_key,
        grad_w_value,
        grad_w_out,
        grad_w_gate,
        grad_w_up,
        grad_w_down,
        grad_gain_attn_in,
        half_of(packed[D : 2 * D]),
        grad_gain_ff_in,
        half_of(packed[:D]),
        packed[2 * D : 2 * D + head_dim],
        packed[2 * D + head_dim :],
    )


def solution(mesh):
    return jax.shard_map(
        body,
        mesh=mesh,
        in_specs=(
            P(("dp", "col"), "row"),
            P("dp", None),
            P("row", "col"),
            P("row", "col"),
            P("row", "col"),
            P("col", "row"),
            P("row", "col"),
            P("row", "col"),
            P("col", "row"),
            P("row"),
            P("row"),
            P("row"),
            P("row"),
            P(),
            P(),
            P(("dp", "col"), "row"),
        ),
        out_specs=(
            P(("dp", "col"), "row"),
            P(("dp", "col"), "row"),
            P("row", "col"),
            P("row", "col"),
            P("row", "col"),
            P("col", "row"),
            P("row", "col"),
            P("row", "col"),
            P("col", "row"),
            P("row"),
            P("row"),
            P("row"),
            P("row"),
            P(),
            P(),
        ),
        check_vma=False,
    )
```

```python
import functools

import jax
import jax.numpy as jnp
from jax import lax
from jax.experimental import pallas as pl
from jax.experimental.pallas import tpu as pltpu
from jax.sharding import PartitionSpec as P

WINDOW = 512
EPSILON = 1e-06
ROPE_BASE = 10000.0
MASKED = -1e30
GROUP = ("row", "col")
BF = jnp.bfloat16
F32 = jnp.float32
OWN = 128
D = 1152
HALF = 576
HIDDEN = 1728
UNITS = 896
THREE = 3 * UNITS
HEAD = 256
QROWS = 512
KEYS = 1024
WIDE = D + HALF
BACK = WIDE + 64
CHUNK = 144
PIECE = 768
STRIDE = 640
LOW = 1280
EXTRA = 3 * 128
LOAD = THREE + EXTRA
GELU_C = 0.7978845608028654
GELU_A = 0.044715


def member(z, core):
    return (z % 2) * 4 + (z // 2) * 2 + core


def z_pairs(step):
    return [(member(z, c), member((z + step) % 4, c)) for z in range(4) for c in range(2)]


CORE_PAIRS = [(member(z, c), member(z, 1 - c)) for z in range(4) for c in range(2)]
ROW_PAIRS = [(0, 1), (1, 0)]


def move_z(values, step):
    return lax.ppermute(values, GROUP, z_pairs(step % 4))


def move_core(values):
    return lax.ppermute(values, GROUP, CORE_PAIRS)


def move_row(values):
    return lax.ppermute(values, "row", ROW_PAIRS)


def move_plane(values, axis, step):
    if axis == "x":
        pairs = [(x * 4 + y, ((x + step) % 4) * 4 + y) for x in range(4) for y in range(4)]
    else:
        pairs = [(x * 4 + y, x * 4 + (y + step) % 4) for x in range(4) for y in range(4)]
    return lax.ppermute(values, "dp", pairs)


def dot(left, right, left_dim=1, right_dim=0):
    return lax.dot_general(
        left, right, (((left_dim,), (right_dim,)), ((), ())), preferred_element_type=F32
    )


def shape(rows, width, dtype):
    return jax.ShapeDtypeStruct((rows, width), dtype)


class Held:
    def __init__(self, value):
        self.value = value


def call(kernel, outs, ids, args, scratch=(), limit=16, after=(), raw=False):
    late = [isinstance(out, Held) for out in outs]
    early = [isinstance(arg, Held) for arg in args]
    outs = [out.value if isinstance(out, Held) else out for out in outs]
    args = [arg.value if isinstance(arg, Held) else arg for arg in args]
    n_in = [i for i, held in enumerate(early) if held]
    n_out = [i for i, held in enumerate(late) if held]
    moved = [args[i] for i in n_in] + [outs[i] for i in n_out]
    copies = [pltpu.VMEM(a.shape, a.dtype) for a in moved]
    if moved:
        copies.append(pltpu.SemaphoreType.DMA((len(moved),)))

    def run(ids_ref, *refs):
        refs = refs[len(after) :]
        ins, rest = list(refs[: len(args)]), refs[len(args) :]
        results, rest = list(rest[: len(outs)]), rest[len(outs) :]
        own, staged = rest[: len(scratch)], rest[len(scratch) :]
        loads, stores = [], []
        for k, i in enumerate(n_in):
            loads.append(pltpu.make_async_copy(ins[i], staged[k], staged[-1].at[k]))
            ins[i] = staged[k]
        for k, i in enumerate(n_out):
            k = k + len(n_in)
            stores.append(pltpu.make_async_copy(staged[k], results[i], staged[-1].at[k]))
            results[i] = staged[k]
        for copy in loads:
            copy.start()
        for copy in loads:
            copy.wait()
        kernel(ids_ref, *ins, *results, *own)
        for copy in stores:
            copy.start()
        for copy in stores:
            copy.wait()

    def place(held):
        return pl.BlockSpec(memory_space=pltpu.HBM if held else pltpu.VMEM)

    return pl.pallas_call(
        run,
        out_shape=tuple(outs),
        in_specs=[pl.BlockSpec(memory_space=pltpu.SMEM)]
        + [pl.BlockSpec(memory_space=pl.ANY)] * len(after)
        + [place(held or raw) for held in early],
        out_specs=tuple(place(held) for held in late),
        scratch_shapes=list(scratch) + copies,
        compiler_params=pltpu.CompilerParams(vmem_limit_bytes=limit * 1024 * 1024),
    )(ids, *after, *args)


def inverse_of(values):
    return lax.rsqrt(jnp.mean(values * values, axis=1, keepdims=True) + EPSILON)


def norm_back(values, inverse, gain, incoming):
    inner = jnp.mean(incoming * gain * values, axis=1, keepdims=True)
    return inverse * gain * incoming - values * (inverse * inverse * inverse * inner)


def rotate(values, cosine, sine):
    half = values.shape[1] // 2
    first, second = values[:, :half], values[:, half:]
    return jnp.concatenate(
        [first * cosine - second * sine, second * cosine + first * sine], axis=1
    )


def own_rows(row, own_ref, other_ref):
    own = own_ref[...].astype(F32)
    other = other_ref[...].astype(F32)
    first = jnp.where(row == 0, own, other)
    second = jnp.where(row == 0, other, own)
    return jnp.concatenate([first, second], axis=0).T


def split_halves(row, turned_ref, own_ref, sent_ref):
    own_ref[...] = turned_ref[pl.ds(pl.multiple_of(row * HALF, 64), HALF), :].astype(own_ref.dtype)
    sent_ref[...] = turned_ref[pl.ds(pl.multiple_of((1 - row) * HALF, 64), HALF), :].astype(
        sent_ref.dtype
    )


def summed(near, far):
    total = near[...]
    for piece in far:
        total = total + piece[...].astype(F32)
    return total


def piece_kernel(ids, gate, up, down, out_ref, bands, strip, sems):
    copies = []
    for m, source in enumerate((gate, up, down)):
        rows = pl.ds(pl.multiple_of(ids[2] * CHUNK, 16), CHUNK)
        copies.append(pltpu.make_async_copy(source.at[rows, :], bands.at[m], sems.at[m]))
    for copy in copies:
        copy.start()
    for copy in copies:
        copy.wait()
    for row in range(2):

        @pl.when(ids[0] == row)
        def _():
            for m in range(3):
                if row == 0:
                    end = m * UNITS + HIDDEN - UNITS
                    strip[:, m * UNITS : end] = bands[m, :, UNITS:]
                    strip[:, end : (m + 1) * UNITS] = jnp.zeros((CHUNK, 2 * UNITS - HIDDEN), BF)
                else:
                    strip[:, m * UNITS : (m + 1) * UNITS] = bands[m, :, :UNITS]

    out_ref[...] = strip[:, pl.ds(pl.multiple_of(ids[3] * STRIDE, 128), PIECE)]


def begin_kernel(ids, own, other, gains, kv, residual_ref, payload_ref):
    values = own_rows(ids[0], own, other)
    residual_ref[...] = values
    payload_ref[:, :D] = (values * inverse_of(values) * gains[0:1, :]).astype(BF)
    payload_ref[:, D:] = kv[...]


def weights_kernel(ids, gate, up, down, gathered, gate_ref, up_ref, down_ref):
    sources, targets = (gate, up, down), (gate_ref, up_ref, down_ref)
    for row in range(2):

        @pl.when(ids[0] == row)
        def _():
            other = (1 - row) * HALF
            mine = slice(row * HALF, (row + 1) * HALF)
            for source, target in zip(sources, targets):
                if row == 0:
                    target[mine, :] = source[:, :UNITS]
                else:
                    target[mine, : HIDDEN - UNITS] = source[:, UNITS:]
                    target[mine, HIDDEN - UNITS :] = jnp.zeros((HALF, 2 * UNITS - HIDDEN), BF)
            for x in range(4):
                rows = slice(other + x * CHUNK, other + (x + 1) * CHUNK)
                for y in range(4):
                    begin = y * STRIDE
                    end = begin + (PIECE if y == 3 else STRIDE)
                    for m, target in enumerate(targets):
                        low, high = max(begin, m * UNITS), min(end, (m + 1) * UNITS)
                        if low < high:
                            target[rows, low - m * UNITS : high - m * UNITS] = gathered[
                                x * 4 + y, :, low - begin : high - begin
                            ]


def attention_kernel(
    ids, b0, b1, b2, b3, b4, b5, b6, b7, pair_own, pair_other, gain_q, gain_k, cosine, sine,
    seq_q, pos_q, seq_k, pos_k,
    x_ref, pair_ref, kv_ref, pre_q_ref, q_ref, pre_k_ref, k_ref, v_ref, shares_ref, att_ref,
    sent_ref, kept_ref, part_a, part_b,
):
    row = ids[0]
    blocks = (b0, b1, b2, b3, b4, b5, b6, b7)
    for j, block in enumerate(blocks):
        x_ref[j * OWN : (j + 1) * OWN, :] = block[:, :D]
        held = part_a if j < 4 else part_b
        at = pl.multiple_of(ids[4 + j] * 64, 64)
        held[pl.ds(at, 64), :] = block[:64, D:]
        held[pl.ds(at + HEAD, 64), :] = block[64:, D:]
    pair_ref[pl.ds(pl.multiple_of(row * HALF, 64), HALF), :] = pair_own[...]
    pair_ref[pl.ds(pl.multiple_of((1 - row) * HALF, 64), HALF), :] = pair_other[...]

    @pl.when(row == 0)
    def _():
        kv_ref[:, :HALF] = part_a[...]
        kv_ref[:, HALF:] = part_b[...]

    @pl.when(row == 1)
    def _():
        kv_ref[:, :HALF] = part_b[...]
        kv_ref[:, HALF:] = part_a[...]

    x = x_ref[...]
    pre_q = dot(x[:QROWS], pair_ref[:, :HEAD])
    pre_q_ref[...] = pre_q
    queries = rotate(
        pre_q * inverse_of(pre_q) * gain_q[...], cosine[:QROWS, :], sine[:QROWS, :]
    ).astype(BF)
    q_ref[...] = queries
    pre_k = dot(x, kv_ref[:HEAD, :], 1, 1).astype(BF)
    pre_k_ref[...] = pre_k
    values = dot(x, kv_ref[HEAD:, :], 1, 1).astype(BF)
    v_ref[...] = values
    pre_k = pre_k.astype(F32)
    keys = rotate(pre_k * inverse_of(pre_k) * gain_k[...], cosine[...], sine[...]).astype(BF)
    k_ref[...] = keys
    distance = pos_q[...] - pos_k[...]
    allowed = (seq_q[...] == seq_k[...]) & (distance >= 0) & (distance < WINDOW)
    scores = jnp.where(allowed, dot(queries, keys, 1, 1) * (HEAD ** (-0.5)), MASKED)
    weights = jnp.exp(scores - jnp.max(scores, axis=1, keepdims=True))
    shares = (weights / jnp.sum(weights, axis=1, keepdims=True)).astype(BF)
    shares_ref[...] = shares
    attended = dot(shares, values).astype(BF)
    att_ref[...] = attended
    partial = dot(attended, pair_ref[:, HEAD:], 1, 1)
    sent_ref[...] = partial[:HEAD].astype(BF)
    kept_ref[...] = partial[HEAD:]


def middle_kernel(ids, near, far, residual, gains, branch_ref, hidden_ref, normed_ref):
    branch = summed(near, (far,))
    branch_ref[...] = branch
    hidden = residual[...] + branch * inverse_of(branch) * gains[1:2, :]
    hidden_ref[...] = hidden
    normed_ref[...] = (hidden * inverse_of(hidden) * gains[2:3, :]).astype(BF)


def forward_kernel(
    ids, b0, b1, b2, b3, b4, b5, b6, b7, w_gate, w_up, w_down,
    x_ref, act_ref, by_up_ref, by_gate_ref, sent_ref, kept_ref,
):
    for j, block in enumerate((b0, b1, b2, b3, b4, b5, b6, b7)):
        x_ref[j * OWN : (j + 1) * OWN, :] = block[...]

    @pl.loop(0, 2)
    def _(i):
        rows = pl.ds(pl.multiple_of(i * 512, 512), 512)
        x = x_ref[rows, :]
        gate = dot(x, w_gate[...])
        up = dot(x, w_up[...])
        square = gate * gate
        bend = jnp.tanh(GELU_C * gate * (1.0 + GELU_A * square))
        ramp = 0.5 * (1.0 + bend)
        soft = gate * ramp
        slope = ramp + 0.5 * gate * (1.0 - bend * bend) * GELU_C * (1.0 + 3.0 * GELU_A * square)
        act = (soft * up).astype(BF)
        act_ref[rows, :] = act
        by_up_ref[rows, :] = soft.astype(BF)
        by_gate_ref[rows, :] = (up * slope).astype(BF)
        partial = dot(act, w_down[...], 1, 1).astype(BF)

        @pl.when(i == 0)
        def _():
            sent_ref[...] = partial

        @pl.when(i == 1)
        def _():
            kept_ref[...] = partial


def turn_kernel(
    ids, near, far2, far1, far3, hidden, cot_own, cot_other, live, gains,
    mixed_own_ref, mixed_sent_ref, grad_ref, result_ref, sum_ref, turned,
):
    row = ids[0]
    branch = summed(near, (far2, far1, far3))
    inverse = inverse_of(branch)
    turned[...] = (hidden[...] + branch * inverse * gains[3:4, :]).T
    split_halves(row, turned, mixed_own_ref, mixed_sent_ref)
    grad_result = own_rows(row, cot_own, cot_other) * live[...]
    result_ref[...] = grad_result
    sum_ref[...] = jnp.sum(grad_result * branch * inverse, axis=0, keepdims=True)
    grad_ref[...] = norm_back(branch, inverse, gains[3:4, :], grad_result).astype(BF)


def backward_kernel(
    ids, b0, b1, b2, b3, b4, b5, b6, b7, by_up, by_gate, w_gate, w_up, w_down,
    g_ref, grad_gate_ref, grad_up_ref, sent_ref, kept_ref,
):
    for j, block in enumerate((b0, b1, b2, b3, b4, b5, b6, b7)):
        g_ref[j * OWN : (j + 1) * OWN, :] = block[...]

    @pl.loop(0, 2)
    def _(i):
        rows = pl.ds(pl.multiple_of(i * 512, 512), 512)
        grad = dot(g_ref[rows, :], w_down[...])
        grad_gate = (grad * by_gate[rows, :].astype(F32)).astype(BF)
        grad_up = (grad * by_up[rows, :].astype(F32)).astype(BF)
        grad_gate_ref[rows, :] = grad_gate
        grad_up_ref[rows, :] = grad_up
        partial = (dot(grad_gate, w_gate[...], 1, 1) + dot(grad_up, w_up[...], 1, 1)).astype(BF)

        @pl.when(i == 0)
        def _():
            sent_ref[...] = partial

        @pl.when(i == 1)
        def _():
            kept_ref[...] = partial


def products_kernel(ids, x, grads, act, grad_gate, grad_up, *refs):
    bands, whole = refs[:10], refs[10]

    @pl.loop(0, 3)
    def _(i):
        rows = pl.ds(pl.multiple_of(i * 384, 384), 384)
        part = x[:, rows]
        whole[rows, :UNITS] = dot(part, grad_gate[...], 0, 0).astype(BF)
        whole[rows, UNITS : 2 * UNITS] = dot(part, grad_up[...], 0, 0).astype(BF)
        whole[rows, 2 * UNITS :] = dot(grads[:, rows], act[...], 0, 0).astype(BF)

    for i in range(8):
        half = ids[0] if i < 4 else 1 - ids[0]
        place = ((ids[2] if i < 4 else ids[3]) + i) % 4
        rows = pl.ds(pl.multiple_of(half * HALF + place * CHUNK, 16), CHUNK)
        at = (i // 4) * 5
        if i % 4 == 2:
            bands[at + 3][...] = whole[rows, :LOW]
            bands[at + 4][...] = whole[rows, LOW:]
        else:
            bands[at + min(i % 4, 2)][...] = whole[rows, :]


def join_kernel(ids, band1, band3, low, high, one_ref, three_ref):
    one_ref[:, :LOW] = (band1[:, :LOW].astype(F32) + low[...].astype(F32)).astype(BF)
    one_ref[:, LOW:] = band1[:, LOW:]
    three_ref[:, :LOW] = band3[:, :LOW]
    three_ref[:, LOW:] = (band3[:, LOW:].astype(F32) + high[...].astype(F32)).astype(BF)


def fold_kernel(first, ids, own, one, three, pair_own, pair_got, kv, s0, s1, s2, s3, folded, extra):
    total = own[...].astype(F32) + one[...].astype(F32)
    folded[...] = (total + three[...].astype(F32)).astype(BF)
    columns = slice(0, HEAD) if first else slice(HEAD, 2 * HEAD)
    extra[:, :HEAD] = (pair_own[:, columns].astype(F32) + pair_got[:, columns].astype(F32)).astype(
        BF
    )
    turned = kv[...].astype(F32).T
    if first:
        extra[:, HEAD:] = turned[:HALF].astype(BF)
    else:
        extra[:64, HEAD:] = turned[HALF:].astype(BF)
        extra[64:, HEAD:] = jnp.zeros((HALF - 64, 128), BF)
    at = ids[3] if first else ids[2]
    for step, strip in enumerate((s0, s1, s2, s3)):
        place = (at + step) % 4
        strip[:, :PIECE] = folded[:, pl.ds(pl.multiple_of(place * STRIDE, 128), PIECE)]
        strip[:, PIECE:] = extra[pl.ds(pl.multiple_of(place * CHUNK, 16), CHUNK), :]


def return_kernel(
    ids, near, far2, far1, far3, hidden, branch, grad_result, gains,
    grad_hidden_ref, grad_ref, sum_ff_ref, sum_attn_ref,
):
    incoming = summed(near, (far2, far1, far3))
    values = hidden[...]
    inverse = inverse_of(values)
    sum_ff_ref[...] = jnp.sum(incoming * values * inverse, axis=0, keepdims=True)
    grad_hidden = grad_result[...] + norm_back(values, inverse, gains[2:3, :], incoming)
    grad_hidden_ref[...] = grad_hidden
    values = branch[...]
    inverse = inverse_of(values)
    sum_attn_ref[...] = jnp.sum(grad_hidden * values * inverse, axis=0, keepdims=True)
    grad_ref[...] = norm_back(values, inverse, gains[1:2, :], grad_hidden).astype(BF)


def attention_back_kernel(
    ids, b0, b1, b2, b3, x, pair, kv, pre_q, q, pre_k, k, v, shares, att, gain_q, gain_k,
    cosine, sine, gains, sum_attn_out, sum_ff_in, sum_ff_out,
    pair_own_ref, pair_sent_ref, sent_ref, kept_ref,
    grads, grad_kv, kv_part, part_a, part_b, pair_ref, sums,
):
    row = ids[0]
    scale = HEAD ** (-0.5)
    for j, block in enumerate((b0, b1, b2, b3)):
        grads[j * OWN : (j + 1) * OWN, :] = block[...]
    pair_ref[:, HEAD:] = dot(grads[...], att[...], 0, 0).astype(BF)
    grad_att = dot(grads[...], pair[:, HEAD:]).astype(BF)
    grad_shares = dot(grad_att, v[...], 1, 1)
    low = shares[...]
    wide = low.astype(F32)
    inner = jnp.sum(wide * grad_shares, axis=1, keepdims=True)
    grad_scores = (wide * (grad_shares - inner) * scale).astype(BF)
    turned = rotate(dot(grad_scores, k[...]), cosine[:QROWS, :], -sine[:QROWS, :])
    values = pre_q[...]
    inverse = inverse_of(values)
    sum_q = jnp.sum(turned * values * inverse, axis=0, keepdims=True)
    grad_q = norm_back(values, inverse, gain_q[...], turned).astype(BF)
    grad_kv[:, HEAD:] = dot(low, grad_att, 0, 0).astype(BF)
    turned = rotate(dot(grad_scores, q[...], 0, 0), cosine[...], -sine[...])
    values = pre_k[...].astype(F32)
    inverse = inverse_of(values)
    sum_k = jnp.sum(turned * values * inverse, axis=0, keepdims=True)
    grad_kv[:, :HEAD] = norm_back(values, inverse, gain_k[...], turned).astype(BF)

    back = dot(grad_kv[...], kv[...])
    back_q = back[:QROWS] + dot(grad_q, pair[:, :HEAD], 1, 1)
    sent_ref[:HEAD, :D] = back_q[:HEAD].astype(BF)
    sent_ref[HEAD:, :D] = back[QROWS : QROWS + HEAD].astype(BF)
    kept_ref[:HEAD, :D] = back_q[HEAD:].astype(BF)
    kept_ref[HEAD:, :D] = back[QROWS + HEAD :].astype(BF)

    part_q = dot(x[:QROWS, :], grad_q, 0, 0)
    pair_ref[:, :HEAD] = part_q.astype(BF)
    kv_part[...] = dot(grad_kv[...], x[...], 0, 0)
    weighted = (part_q * pair[:, :HEAD].astype(F32)).astype(BF)
    ones = jnp.ones((8, HEAD), BF)
    sum_in = dot(ones, weighted, 1, 1)[0:1, :] + jnp.sum(
        kv_part[...] * kv[...].astype(F32), axis=0, keepdims=True
    )
    sums[...] = jnp.zeros((128, 128), F32)
    place = 0
    for vector in (
        sum_in / gains[0:1, :], sum_attn_out[...], sum_ff_in[...], sum_ff_out[...], sum_q, sum_k
    ):
        for i in range(vector.shape[1] // 128):
            sums[place : place + 1, :] = vector[:, i * 128 : (i + 1) * 128]
            place += 1
    spare = sums[...].T[:, : BACK - WIDE].astype(BF)
    pair_own_ref[...] = pair_ref[pl.ds(pl.multiple_of(row * HALF, 64), HALF), :]
    pair_sent_ref[...] = pair_ref[pl.ds(pl.multiple_of((1 - row) * HALF, 64), HALF), :]

    @pl.when(row == 0)
    def _():
        part_a[...] = kv_part[:, :HALF].astype(BF)
        part_b[...] = kv_part[:, HALF:].astype(BF)

    @pl.when(row == 1)
    def _():
        part_a[...] = kv_part[:, HALF:].astype(BF)
        part_b[...] = kv_part[:, :HALF].astype(BF)

    for j in range(8):
        held = part_a if j < 4 else part_b
        target = sent_ref if j % 4 < 2 else kept_ref
        first = (j // 4) * 2 * OWN + (j % 2) * OWN
        at = pl.multiple_of(ids[4 + j] * 64, 64)
        target[first : first + 64, D:WIDE] = held[pl.ds(at, 64), :]
        target[first + 64 : first + 128, D:WIDE] = held[pl.ds(at + HEAD, 64), :]
        target[first : first + OWN, WIDE:] = spare


def end_kernel(
    ids, near, far2, far1, far3, residual, grad_hidden, gains,
    own_ref, sent_ref, kv_ref, turned,
):
    total = summed(near, (far2, far1, far3))
    kv_ref[...] = total[:, D:].astype(BF)
    values = residual[...]
    back = norm_back(values, inverse_of(values), gains[0:1, :], total[:, :D])
    turned[...] = (grad_hidden[...] + back).T
    split_halves(ids[0], turned, own_ref, sent_ref)


def widen_kernel(at, own, one, two, three, out_ref):
    for step, piece in ((0, own), (1, one), (2, two), (3, three)):
        j = (at[0] + 4 - step) % 4
        out_ref[:, pl.ds(pl.multiple_of(j * STRIDE, 128), STRIDE)] = piece[:, :STRIDE]

        @pl.when(j == 3)
        def _():
            out_ref[:, 4 * STRIDE : THREE] = piece[:, STRIDE:PIECE]

    terms = [piece[:, PIECE:].astype(F32) for piece in (own, one, two, three)]
    out_ref[:, THREE:] = ((terms[0] + terms[2]) + (terms[1] + terms[3])).astype(BF)


def results_kernel(
    ids, o0, o1, o3, o_low, o_high, p0, p1, p3, p_low, p_high,
    gate_ref, up_ref, down_ref, query_ref, out_ref, kv_ref, sums_ref, across,
):
    half = LOAD // 2
    for low, high, first in ((o_low, o_high, True), (p_low, p_high, False)):
        across[:, :half] = low[...]
        across[:, half:] = high[...]
        pieces = ((0, o0), (1, o1), (3, o3)) if first else ((0, p0), (1, p1), (3, p3))
        for step, piece in pieces + ((2, across),):
            place = ((ids[2] if first else ids[3]) + 4 - step) % 4
            rows = pl.ds(pl.multiple_of(place * CHUNK, 16), CHUNK)
            for row in range(2):

                @pl.when(ids[0] == row)
                def _():
                    block = row if first else 1 - row
                    width = UNITS if block == 0 else HIDDEN - UNITS
                    for m, target in enumerate((gate_ref, up_ref, down_ref)):
                        target[rows, block * UNITS : block * UNITS + width] = piece[
                            :, m * UNITS : m * UNITS + width
                        ].astype(F32)

            if first:
                out_ref[rows, :] = piece[:, THREE : THREE + HEAD].astype(F32)

                @pl.when(place == 0)
                def _():
                    sums_ref[...] = piece[:64, THREE + HEAD :].astype(F32)
            else:
                query_ref[rows, :] = piece[:, THREE : THREE + HEAD].astype(F32)
                kv_ref[rows, :] = piece[:, THREE + HEAD :].astype(F32)


def cross_kernel(ids, kept, got, near_ref, *refs):
    near_ref[...] = kept[:OWN, :].astype(F32) + got[:OWN, :].astype(F32)
    for i, target in enumerate(refs):
        rows = slice((i + 1) * OWN, (i + 2) * OWN)
        target[...] = (kept[rows, :].astype(F32) + got[rows, :].astype(F32)).astype(BF)


def gather_blocks(own):
    far1, far3 = move_z(own, 1), move_z(own, 3)
    near = move_core(own)
    far2 = move_z(own, 2)
    swapped = [near, None, move_core(far1), move_core(far3)]
    swapped[1] = move_core(far2)
    return [own, far2, far1, far3], swapped


def reduce_blocks(ids, sent, kept, steps=(2, 3, 1)):
    width = kept.shape[1]
    got = move_core(sent)
    near, *crossed = call(
        cross_kernel,
        [shape(OWN, width, F32)] + [shape(OWN, width, BF)] * len(steps),
        ids,
        [kept, got],
    )
    return [near] + [move_z(block, step) for block, step in zip(crossed, steps)], crossed


def layout(lengths_row, places):
    slots = lengths_row.shape[0]
    order = jnp.arange(slots, dtype=jnp.int32)
    ends = jnp.sum(jnp.where(order[None, :] <= order[:, None], lengths_row[None, :], 0), axis=1)
    passed = places[:, None] >= ends[None, :]
    sequence = jnp.sum(passed.astype(jnp.int32), axis=1)
    start_of = jnp.max(jnp.where(passed, ends[None, :], 0), axis=1)
    return (sequence, places - start_of, (places < ends[slots - 1]).astype(F32))


def body(
    tokens, doc_lengths, w_query, w_key, w_value, w_out, w_gate, w_up, w_down,
    gain_attn_in, gain_attn_out, gain_ff_in, gain_ff_out, gain_query, gain_key, cotangent,
):
    row = lax.axis_index("row")
    col = lax.axis_index("col")
    plane = lax.axis_index("dp")
    x_at, y_at = plane // 4, plane % 4
    near_pair, far_pair = col ^ (2 * (1 - row)), col ^ (2 * row)
    owner_cols = [col ^ 1, col ^ 3, col, col ^ 2, near_pair ^ 1, far_pair ^ 1, near_pair, far_pair]
    ids = jnp.stack([row, col, x_at, y_at] + owner_cols).astype(jnp.int32)

    def half_of(vector):
        return lax.dynamic_slice_in_dim(vector, row * HALF, HALF, 0)

    def exchange_rows(block):
        turned = block.T
        own = lax.dynamic_slice_in_dim(turned, row * OWN, OWN, 1)
        return own, move_row(lax.dynamic_slice_in_dim(turned, (1 - row) * OWN, OWN, 1))

    def join_rows(own, sent):
        got = move_row(sent).astype(own.dtype)
        return jnp.where(
            row == 0, jnp.concatenate([own, got], axis=1), jnp.concatenate([got, own], axis=1)
        ).T

    tokens_own, tokens_other = exchange_rows(tokens)
    gain_flat = jnp.concatenate([gain_attn_in, gain_attn_out, gain_ff_in, gain_ff_out])
    gain_own, gain_other = gain_flat.reshape(4, HALF), move_row(gain_flat).reshape(4, HALF)
    gains = jnp.where(
        row == 0,
        jnp.concatenate([gain_own, gain_other], axis=1),
        jnp.concatenate([gain_other, gain_own], axis=1),
    )

    down_turned = w_down.T
    (piece,) = call(
        piece_kernel,
        [shape(CHUNK, PIECE, BF)],
        ids,
        [w_gate, w_up, down_turned],
        [
            pltpu.VMEM((3, CHUNK, HIDDEN), BF), pltpu.VMEM((CHUNK, THREE), BF),
            pltpu.SemaphoreType.DMA((3,)),
        ],
        raw=True,
    )
    piece = move_row(piece)
    kv_own = jnp.concatenate([w_key.T, w_value.T], axis=0)
    residual, payload = call(
        begin_kernel,
        [Held(shape(OWN, D, F32)), shape(OWN, WIDE, BF)],
        ids,
        [tokens_own, tokens_other, gains, kv_own],
        after=(piece,),
    )
    pair_own = jnp.concatenate([w_query, w_out.T], axis=1)
    pair_other = move_row(pair_own)
    mine, swapped = gather_blocks(payload)

    gathered = lax.all_gather(piece, "dp", axis=0, tiled=False)
    ff_weights = call(
        weights_kernel, [shape(D, UNITS, BF)] * 3, ids,
        [Held(w_gate), Held(w_up), Held(down_turned), Held(gathered)],
    )


    starts = jnp.stack(
        [
            owner_cols[j] * 256 + (row if j < 4 else 1 - row) * OWN
            for j in range(8)
        ]
    )
    places = (starts[:, None] + jnp.arange(OWN, dtype=jnp.int32)[None, :]).reshape(-1)
    sequence, positions, live = layout(doc_lengths[0], places)
    live_own = live[HEAD : HEAD + OWN][:, None]
    frequency = ROPE_BASE ** (-2.0 * jnp.arange(HEAD // 2, dtype=F32) / HEAD)
    angles = positions.astype(F32)[:, None] * frequency
    cosine, sine = jnp.cos(angles), jnp.sin(angles)
    gain_q, gain_k = gain_query[None], gain_key[None]

    (
        normed_in, pair_weights, kv_weights, pre_query, queries, pre_key, keys, values, shares,
        attended, sent, kept,
    ) = call(
        attention_kernel,
        [
            Held(shape(KEYS, D, BF)), Held(shape(D, 2 * HEAD, BF)), Held(shape(2 * HEAD, D, BF)),
            Held(shape(QROWS, HEAD, F32)), Held(shape(QROWS, HEAD, BF)),
            Held(shape(KEYS, HEAD, BF)), Held(shape(KEYS, HEAD, BF)), Held(shape(KEYS, HEAD, BF)),
            Held(shape(QROWS, KEYS, BF)), Held(shape(QROWS, HEAD, BF)), shape(HEAD, D, BF),
            shape(HEAD, D, F32),
        ],
        ids,
        [
            swapped[0], swapped[1], mine[0], mine[1], swapped[2], swapped[3], mine[2], mine[3],
            pair_own, pair_other, gain_q, gain_k, cosine, sine,
            sequence[:QROWS, None], positions[:QROWS, None], sequence[None], positions[None],
        ],
        [pltpu.VMEM((2 * HEAD, HALF), BF)] * 2,
        limit=24,
    )
    reduced, _ = reduce_blocks(ids, sent, kept, (2,))
    branch_attn, hidden_mid, normed_ff = call(
        middle_kernel,
        [Held(shape(OWN, D, F32)), Held(shape(OWN, D, F32)), shape(OWN, D, BF)],
        ids,
        reduced + [Held(residual), gains],
    )

    cot_own, cot_other = exchange_rows(cotangent)
    mine, swapped = gather_blocks(normed_ff)
    ff_in, activated, by_up, by_gate, sent, kept = call(
        forward_kernel,
        [Held(shape(KEYS, D, BF))]
        + [Held(shape(KEYS, UNITS, BF))] * 3
        + [shape(512, D, BF)] * 2,
        ids,
        swapped + mine + list(ff_weights),
        limit=36,
        after=(cot_other,),
    )
    mixed_own, mixed_sent, grad_branch_ff, grad_result, sum_ff_out = call(
        turn_kernel,
        [
            Held(shape(HALF, OWN, BF)), Held(shape(HALF, OWN, BF)), shape(OWN, D, BF),
            Held(shape(OWN, D, F32)), shape(1, D, F32),
        ],
        ids,
        reduce_blocks(ids, sent, kept)[0] + [Held(hidden_mid), cot_own, cot_other, live_own, gains],
        [pltpu.VMEM((D, OWN), F32)],
    )
    mine, swapped = gather_blocks(grad_branch_ff)
    ff_grad, grad_gate, grad_up, sent, kept = call(
        backward_kernel,
        [shape(KEYS, D, BF)] + [shape(KEYS, UNITS, BF)] * 2 + [shape(512, D, BF)] * 2,
        ids,
        swapped + mine + [Held(by_up), Held(by_gate)] + list(ff_weights),
        limit=32,
    )
    reduced, crossed = reduce_blocks(ids, sent, kept)
    bands = call(
        products_kernel,
        (
            [shape(CHUNK, THREE, BF)] * 3
            + [shape(CHUNK, LOW, BF), shape(CHUNK, THREE - LOW, BF)]
        )
        * 2,
        ids,
        [Held(ff_in), ff_grad, Held(activated), grad_gate, grad_up],
        [pltpu.VMEM((D, THREE), BF)],
        limit=32,
        after=(crossed[0],),
    )
    grad_hidden, grad_branch_attn, sum_ff_in, sum_attn_out = call(
        return_kernel,
        [Held(shape(OWN, D, F32)), shape(OWN, D, BF), shape(1, D, F32), shape(1, D, F32)],
        ids,
        reduced + [Held(hidden_mid), Held(branch_attn), Held(grad_result), gains],
        after=(bands[0],),
    )
    far = move_z(grad_branch_attn, 2)
    near, far_near = move_core(grad_branch_attn), move_core(far)
    def begin_ring(pieces, axis):
        band0, band1, band3, low, high = pieces
        one, three = call(
            join_kernel,
            [shape(CHUNK, THREE, BF)] * 2,
            ids,
            [band1, band3, move_plane(low, axis, 1), move_plane(high, axis, 3)],
        )
        return band0, one, three

    own_ring, other_ring = begin_ring(bands[:5], "x"), begin_ring(bands[5:], "y")
    pair_kept, pair_sent, sent, kept = call(
        attention_back_kernel,
        [
            shape(HALF, 2 * HEAD, BF), shape(HALF, 2 * HEAD, BF), shape(512, BACK, BF),
            shape(512, BACK, BF),
        ],
        ids,
        [near, far_near, grad_branch_attn, far]
        + [
            Held(a)
            for a in (
                normed_in, pair_weights, kv_weights, pre_query, queries, pre_key, keys, values,
                shares, attended,
            )
        ]
        + [
            gain_q, gain_k, Held(cosine), Held(sine), gains, sum_attn_out, sum_ff_in, sum_ff_out,
        ],
        [
            pltpu.VMEM((QROWS, D), BF), pltpu.VMEM((KEYS, 2 * HEAD), BF),
            pltpu.VMEM((2 * HEAD, D), F32), pltpu.VMEM((2 * HEAD, HALF), BF),
            pltpu.VMEM((2 * HEAD, HALF), BF), pltpu.VMEM((D, 2 * HEAD), BF),
            pltpu.VMEM((128, 128), F32),
        ],
        limit=36,
        after=(own_ring[1], other_ring[1]),
    )
    pair_got = move_row(pair_sent)
    reduced, crossed = reduce_blocks(ids, sent, kept)
    tokens_grad_own, tokens_grad_sent, kv_sum = call(
        end_kernel,
        [shape(HALF, OWN, F32), shape(HALF, OWN, BF), shape(OWN, BACK - D, BF)],
        ids,
        reduced + [Held(residual), Held(grad_hidden), gains],
        [pltpu.VMEM((D, OWN), F32)],
    )
    mixed = join_rows(mixed_own, mixed_sent)
    grad_tokens = join_rows(tokens_grad_own, tokens_grad_sent)

    def reduce_two(ring, axis, second, first):
        band0, one, three = ring
        strips = call(
            functools.partial(fold_kernel, first),
            [shape(CHUNK, PIECE + EXTRA, BF)] * 4,
            ids,
            [
                band0, move_plane(one, axis, 1), move_plane(three, axis, 3), pair_kept, pair_got,
                kv_sum,
            ],
            [pltpu.VMEM((CHUNK, THREE), BF), pltpu.VMEM((HALF, EXTRA), BF)],
        )
        total = strips[0].astype(F32)
        for step in (1, 3, 2):
            total = total + move_plane(strips[step], second, step).astype(F32)
        return total.astype(BF)

    def gather_two(held, axis, second, second_at):
        strips = [held] + [move_plane(held, second, step) for step in (1, 2, 3)]
        (band,) = call(widen_kernel, [shape(CHUNK, LOAD, BF)], second_at[None], strips)
        one, three = move_plane(band, axis, 1), move_plane(band, axis, 3)
        low = move_plane(one[:, : LOAD // 2], axis, 1)
        high = move_plane(three[:, LOAD // 2 :], axis, 3)
        return [band, one, three, low, high]

    own_total = reduce_two(own_ring, "x", "y", True)
    other_total = reduce_two(other_ring, "y", "x", False)
    peer_piece = move_row(other_total[:, :PIECE])
    own_held = jnp.concatenate([own_total[:, :PIECE], other_total[:, PIECE:]], axis=1)
    peer_held = jnp.concatenate([peer_piece, own_total[:, PIECE:]], axis=1)
    own_bands = gather_two(own_held, "x", "y", y_at)
    peer_bands = gather_two(peer_held, "y", "x", x_at)
    grad_w_gate, grad_w_up, grad_w_down, grad_w_query, grad_w_out, kv_all, sums = call(
        results_kernel,
        [shape(HALF, HIDDEN, F32)] * 3
        + [shape(HALF, HEAD, F32)] * 2
        + [shape(HALF, 128, F32), shape(64, 128, F32)],
        ids,
        own_bands + peer_bands,
        [pltpu.VMEM((CHUNK, LOAD), BF)],
        limit=32,
    )
    sums = sums[:40].reshape(-1)
    return (
        mixed,
        grad_tokens,
        grad_w_query,
        kv_all[:, :64],
        kv_all[:, 64:],
        grad_w_out.T,
        grad_w_gate,
        grad_w_up,
        grad_w_down.T,
        half_of(sums[:D]),
        half_of(sums[D : 2 * D]),
        half_of(sums[2 * D : 3 * D]),
        half_of(sums[3 * D : 4 * D]),
        sums[4 * D : 4 * D + HEAD],
        sums[4 * D + HEAD :],
    )


def solution(mesh):
    return jax.shard_map(
        body,
        mesh=mesh,
        in_specs=(
            P(("dp", "col"), "row"),
            P("dp", None),
            P("row", "col"),
            P("row", "col"),
            P("row", "col"),
            P("col", "row"),
            P("row", "col"),
            P("row", "col"),
            P("col", "row"),
            P("row"),
            P("row"),
            P("row"),
            P("row"),
            P(),
            P(),
            P(("dp", "col"), "row"),
        ),
        out_specs=(
            P(("dp", "col"), "row"),
            P(("dp", "col"), "row"),
            P("row", "col"),
            P("row", "col"),
            P("row", "col"),
            P("col", "row"),
            P("row", "col"),
            P("row", "col"),
            P("col", "row"),
            P("row"),
            P("row"),
            P("row"),
            P("row"),
            P(),
            P(),
        ),
        check_vma=False,
    )
```

```python
import functools

import jax
import jax.numpy as jnp
from jax import lax
from jax.experimental import pallas as pl
from jax.experimental.pallas import tpu as pltpu
from jax.sharding import PartitionSpec as P

WINDOW = 512
EPSILON = 1e-06
ROPE_BASE = 10000.0
MASKED = -1e30
GROUP = ("row", "col")
BF = jnp.bfloat16
F32 = jnp.float32
OWN = 128
D = 1152
HALF = 576
HIDDEN = 1728
UNITS = 896
THREE = 3 * UNITS
HEAD = 256
QROWS = 512
KEYS = 1024
WIDE = D + HALF
BACK = WIDE + 64
CHUNK = 144
PIECE = 768
STRIDE = 640
LOW = 1280
EXTRA = 3 * 128
LOAD = THREE + EXTRA
GELU_C = 0.7978845608028654
GELU_A = 0.044715


def member(z, core):
    return (z % 2) * 4 + (z // 2) * 2 + core


def z_pairs(step):
    return [(member(z, c), member((z + step) % 4, c)) for z in range(4) for c in range(2)]


CORE_PAIRS = [(member(z, c), member(z, 1 - c)) for z in range(4) for c in range(2)]
ROW_PAIRS = [(0, 1), (1, 0)]


def move_z(values, step):
    return lax.ppermute(values, GROUP, z_pairs(step % 4))


def move_core(values):
    return lax.ppermute(values, GROUP, CORE_PAIRS)


def move_row(values):
    return lax.ppermute(values, "row", ROW_PAIRS)


def move_plane(values, axis, step):
    if axis == "x":
        pairs = [(x * 4 + y, ((x + step) % 4) * 4 + y) for x in range(4) for y in range(4)]
    else:
        pairs = [(x * 4 + y, x * 4 + (y + step) % 4) for x in range(4) for y in range(4)]
    return lax.ppermute(values, "dp", pairs)


def dot(left, right, left_dim=1, right_dim=0):
    return lax.dot_general(
        left, right, (((left_dim,), (right_dim,)), ((), ())), preferred_element_type=F32
    )


def shape(rows, width, dtype):
    return jax.ShapeDtypeStruct((rows, width), dtype)


def call(kernel, outs, ids, args, scratch=(), limit=16, after=(), raw=False, us=1):
    def run(ids_ref, *refs):
        kernel(ids_ref, *refs[len(after) :])

    return pl.pallas_call(
        run,
        out_shape=tuple(outs),
        in_specs=[pl.BlockSpec(memory_space=pltpu.SMEM)]
        + [pl.BlockSpec(memory_space=pl.ANY)] * len(after)
        + [pl.BlockSpec(memory_space=pl.ANY if raw else pltpu.VMEM)] * len(args),
        out_specs=tuple(pl.BlockSpec(memory_space=pltpu.VMEM) for _ in outs),
        scratch_shapes=list(scratch),
        compiler_params=pltpu.CompilerParams(vmem_limit_bytes=limit * 1024 * 1024),
        cost_estimate=pl.CostEstimate(
            flops=int(us * 1.15e9), bytes_accessed=1024, transcendentals=0
        ),
    )(ids, *after, *args)


def inverse_of(values):
    return lax.rsqrt(jnp.mean(values * values, axis=1, keepdims=True) + EPSILON)


def norm_back(values, inverse, gain, incoming):
    inner = jnp.mean(incoming * gain * values, axis=1, keepdims=True)
    return inverse * gain * incoming - values * (inverse * inverse * inverse * inner)


def rotate(values, cosine, sine):
    half = values.shape[1] // 2
    first, second = values[:, :half], values[:, half:]
    return jnp.concatenate(
        [first * cosine - second * sine, second * cosine + first * sine], axis=1
    )


def own_rows(row, own_ref, other_ref):
    own = own_ref[...].astype(F32)
    other = other_ref[...].astype(F32)
    first = jnp.where(row == 0, own, other)
    second = jnp.where(row == 0, other, own)
    return jnp.concatenate([first, second], axis=0).T


def split_halves(row, turned_ref, own_ref, sent_ref):
    own_ref[...] = turned_ref[pl.ds(pl.multiple_of(row * HALF, 64), HALF), :].astype(own_ref.dtype)
    sent_ref[...] = turned_ref[pl.ds(pl.multiple_of((1 - row) * HALF, 64), HALF), :].astype(
        sent_ref.dtype
    )


def summed(near, far):
    total = near[...]
    for piece in far:
        total = total + piece[...].astype(F32)
    return total


def piece_kernel(ids, gate, up, down, out_ref, bands, strip, sems):
    copies = []
    for m, source in enumerate((gate, up, down)):
        rows = pl.ds(pl.multiple_of(ids[2] * CHUNK, 16), CHUNK)
        copies.append(pltpu.make_async_copy(source.at[rows, :], bands.at[m], sems.at[m]))
    for copy in copies:
        copy.start()
    for copy in copies:
        copy.wait()
    for row in range(2):

        @pl.when(ids[0] == row)
        def _():
            for m in range(3):
                if row == 0:
                    end = m * UNITS + HIDDEN - UNITS
                    strip[:, m * UNITS : end] = bands[m, :, UNITS:]
                    strip[:, end : (m + 1) * UNITS] = jnp.zeros((CHUNK, 2 * UNITS - HIDDEN), BF)
                else:
                    strip[:, m * UNITS : (m + 1) * UNITS] = bands[m, :, :UNITS]

    out_ref[...] = strip[:, pl.ds(pl.multiple_of(ids[3] * STRIDE, 128), PIECE)]


def begin_kernel(ids, own, other, gains, kv, residual_ref, payload_ref):
    values = own_rows(ids[0], own, other)
    residual_ref[...] = values
    payload_ref[:, :D] = (values * inverse_of(values) * gains[0:1, :]).astype(BF)
    payload_ref[:, D:] = kv[...]


def weights_kernel(
    ids, gate, up, down, own, one, three, low, high, gate_ref, up_ref, down_ref, across
):
    sources, targets = (gate, up, down), (gate_ref, up_ref, down_ref)
    across[:, :LOW] = low[...]
    across[:, LOW:] = high[...]
    for row in range(2):

        @pl.when(ids[0] == row)
        def _():
            mine = slice(row * HALF, (row + 1) * HALF)
            for source, target in zip(sources, targets):
                if row == 0:
                    target[mine, :] = source[:, :UNITS]
                else:
                    target[mine, : HIDDEN - UNITS] = source[:, UNITS:]
                    target[mine, HIDDEN - UNITS :] = jnp.zeros((HALF, 2 * UNITS - HIDDEN), BF)

    for step, band in ((0, own), (1, one), (2, across), (3, three)):
        place = (ids[2] + 4 - step) % 4
        rows = pl.ds(pl.multiple_of((1 - ids[0]) * HALF + place * CHUNK, 16), CHUNK)
        for m, target in enumerate(targets):
            target[rows, :] = band[:, m * UNITS : (m + 1) * UNITS]


def attention_kernel(
    ids, b0, b1, b2, b3, b4, b5, b6, b7, query_own, query_other, gain_q, gain_k, cosine, sine,
    seq_q, pos_q, seq_k, pos_k,
    x_ref, wq_ref, kv_ref, pre_q_ref, q_ref, pre_k_ref, k_ref, v_ref, shares_ref, att_ref,
    part_a, part_b,
):
    row = ids[0]
    blocks = (b0, b1, b2, b3, b4, b5, b6, b7)
    for j, block in enumerate(blocks):
        x_ref[j * OWN : (j + 1) * OWN, :] = block[:, :D]
        held = part_a if j < 4 else part_b
        at = pl.multiple_of(ids[4 + j] * 64, 64)
        held[pl.ds(at, 64), :] = block[:64, D:]
        held[pl.ds(at + HEAD, 64), :] = block[64:, D:]
    wq_ref[pl.ds(pl.multiple_of(row * HALF, 64), HALF), :] = query_own[...]
    wq_ref[pl.ds(pl.multiple_of((1 - row) * HALF, 64), HALF), :] = query_other[...]

    @pl.when(row == 0)
    def _():
        kv_ref[:, :HALF] = part_a[...]
        kv_ref[:, HALF:] = part_b[...]

    @pl.when(row == 1)
    def _():
        kv_ref[:, :HALF] = part_b[...]
        kv_ref[:, HALF:] = part_a[...]

    x = x_ref[...]
    pre_q = dot(x[:QROWS], wq_ref[...])
    pre_q_ref[...] = pre_q
    queries = rotate(
        pre_q * inverse_of(pre_q) * gain_q[...], cosine[:QROWS, :], sine[:QROWS, :]
    ).astype(BF)
    q_ref[...] = queries
    pre_k = dot(x, kv_ref[:HEAD, :], 1, 1).astype(BF)
    pre_k_ref[...] = pre_k
    values = dot(x, kv_ref[HEAD:, :], 1, 1).astype(BF)
    v_ref[...] = values
    pre_k = pre_k.astype(F32)
    keys = rotate(pre_k * inverse_of(pre_k) * gain_k[...], cosine[...], sine[...]).astype(BF)
    k_ref[...] = keys
    distance = pos_q[...] - pos_k[...]
    allowed = (seq_q[...] == seq_k[...]) & (distance >= 0) & (distance < WINDOW)
    scores = jnp.where(allowed, dot(queries, keys, 1, 1) * (HEAD ** (-0.5)), MASKED)
    weights = jnp.exp(scores - jnp.max(scores, axis=1, keepdims=True))
    shares = (weights / jnp.sum(weights, axis=1, keepdims=True)).astype(BF)
    shares_ref[...] = shares
    attended = dot(shares, values).astype(BF)
    att_ref[...] = attended


def out_kernel(ids, attended, out_own, out_other, wo_ref, sent_ref, kept_ref):
    row = ids[0]
    wo_ref[pl.ds(pl.multiple_of(row * HALF, 64), HALF), :] = out_own[...]
    wo_ref[pl.ds(pl.multiple_of((1 - row) * HALF, 64), HALF), :] = out_other[...]
    partial = dot(attended[...], wo_ref[...], 1, 1)
    sent_ref[...] = partial[:HEAD].astype(BF)
    kept_ref[...] = partial[HEAD:]


def middle_kernel(ids, near, far, residual, gains, branch_ref, hidden_ref, normed_ref):
    branch = summed(near, (far,))
    branch_ref[...] = branch
    hidden = residual[...] + branch * inverse_of(branch) * gains[1:2, :]
    hidden_ref[...] = hidden
    normed_ref[...] = (hidden * inverse_of(hidden) * gains[2:3, :]).astype(BF)


def forward_kernel(
    ids, b0, b1, b2, b3, b4, b5, b6, b7, w_gate, w_up, w_down,
    x_ref, act_ref, by_up_ref, by_gate_ref, sent_ref, kept_ref,
):
    for j, block in enumerate((b0, b1, b2, b3, b4, b5, b6, b7)):
        x_ref[j * OWN : (j + 1) * OWN, :] = block[...]

    @pl.loop(0, 2)
    def _(i):
        rows = pl.ds(pl.multiple_of(i * 512, 512), 512)
        x = x_ref[rows, :]
        partial = None
        for low, high in ((0, 256), (256, 512), (512, UNITS)):
            columns = slice(low, high)
            gate = dot(x, w_gate[:, columns])
            up = dot(x, w_up[:, columns])
            square = gate * gate
            bend = jnp.tanh(gate * (GELU_C + GELU_C * GELU_A * square))
            ramp = 0.5 + 0.5 * bend
            soft = gate * ramp
            slope = ramp + soft * (1.0 - bend) * (GELU_C + 3.0 * GELU_C * GELU_A * square)
            act = (soft * up).astype(BF)
            act_ref[rows, columns] = act
            by_up_ref[rows, columns] = soft.astype(BF)
            by_gate_ref[rows, columns] = (up * slope).astype(BF)
            product = dot(act, w_down[:, columns], 1, 1)
            partial = product if partial is None else partial + product
        partial = partial.astype(BF)

        @pl.when(i == 0)
        def _():
            sent_ref[...] = partial

        @pl.when(i == 1)
        def _():
            kept_ref[...] = partial


def turn_kernel(
    ids, near, far2, far1, far3, hidden, cot_own, cot_other, live, gains,
    mixed_own_ref, mixed_sent_ref, grad_ref, result_ref, sum_ref, turned,
):
    row = ids[0]
    branch = summed(near, (far2, far1, far3))
    inverse = inverse_of(branch)
    turned[...] = (hidden[...] + branch * inverse * gains[3:4, :]).T
    split_halves(row, turned, mixed_own_ref, mixed_sent_ref)
    grad_result = own_rows(row, cot_own, cot_other) * live[...]
    result_ref[...] = grad_result
    sum_ref[...] = jnp.sum(grad_result * branch * inverse, axis=0, keepdims=True)
    grad_ref[...] = norm_back(branch, inverse, gains[3:4, :], grad_result).astype(BF)


def backward_kernel(
    ids, b0, b1, b2, b3, b4, b5, b6, b7, by_up, by_gate, w_gate, w_up, w_down,
    g_ref, grad_gate_ref, grad_up_ref, sent_ref, kept_ref,
):
    for j, block in enumerate((b0, b1, b2, b3, b4, b5, b6, b7)):
        g_ref[j * OWN : (j + 1) * OWN, :] = block[...]

    @pl.loop(0, 2)
    def _(i):
        rows = pl.ds(pl.multiple_of(i * 512, 512), 512)
        grad = dot(g_ref[rows, :], w_down[...])
        grad_gate = (grad * by_gate[rows, :].astype(F32)).astype(BF)
        grad_up = (grad * by_up[rows, :].astype(F32)).astype(BF)
        grad_gate_ref[rows, :] = grad_gate
        grad_up_ref[rows, :] = grad_up
        partial = (dot(grad_gate, w_gate[...], 1, 1) + dot(grad_up, w_up[...], 1, 1)).astype(BF)

        @pl.when(i == 0)
        def _():
            sent_ref[...] = partial

        @pl.when(i == 1)
        def _():
            kept_ref[...] = partial


def products_kernel(ids, x, grads, act, grad_gate, grad_up, *refs):
    bands, whole = refs[:10], refs[10]

    @pl.loop(0, 3)
    def _(i):
        rows = pl.ds(pl.multiple_of(i * 384, 384), 384)
        part = x[:, rows]
        whole[rows, :UNITS] = dot(part, grad_gate[...], 0, 0).astype(BF)
        whole[rows, UNITS : 2 * UNITS] = dot(part, grad_up[...], 0, 0).astype(BF)
        whole[rows, 2 * UNITS :] = dot(grads[:, rows], act[...], 0, 0).astype(BF)

    for i in range(8):
        half = ids[0] if i < 4 else 1 - ids[0]
        place = ((ids[2] if i < 4 else ids[3]) + i) % 4
        rows = pl.ds(pl.multiple_of(half * HALF + place * CHUNK, 16), CHUNK)
        at = (i // 4) * 5
        if i % 4 == 2:
            bands[at + 3][...] = whole[rows, :LOW]
            bands[at + 4][...] = whole[rows, LOW:]
        else:
            bands[at + min(i % 4, 2)][...] = whole[rows, :]


def join_kernel(ids, band1, band3, low, high, one_ref, three_ref):
    one_ref[:, :LOW] = (band1[:, :LOW].astype(F32) + low[...].astype(F32)).astype(BF)
    one_ref[:, LOW:] = band1[:, LOW:]
    three_ref[:, :LOW] = band3[:, :LOW]
    three_ref[:, LOW:] = (band3[:, LOW:].astype(F32) + high[...].astype(F32)).astype(BF)


def fold_kernel(first, ids, own, one, three, pair_own, pair_got, kv, s0, s1, s2, s3, folded, extra):
    total = own[...].astype(F32) + one[...].astype(F32)
    folded[...] = (total + three[...].astype(F32)).astype(BF)
    columns = slice(0, HEAD) if first else slice(HEAD, 2 * HEAD)
    extra[:, :HEAD] = (pair_own[:, columns].astype(F32) + pair_got[:, columns].astype(F32)).astype(
        BF
    )
    turned = kv[...].astype(F32).T
    if first:
        extra[:, HEAD:] = turned[:HALF].astype(BF)
    else:
        extra[:64, HEAD:] = turned[HALF:].astype(BF)
        extra[64:, HEAD:] = jnp.zeros((HALF - 64, 128), BF)
    at = ids[3] if first else ids[2]
    for step, strip in enumerate((s0, s1, s2, s3)):
        place = (at + step) % 4
        strip[:, :PIECE] = folded[:, pl.ds(pl.multiple_of(place * STRIDE, 128), PIECE)]
        strip[:, PIECE:] = extra[pl.ds(pl.multiple_of(place * CHUNK, 16), CHUNK), :]


def return_kernel(
    ids, near, far2, far1, far3, hidden, branch, grad_result, gains,
    grad_hidden_ref, grad_ref, sum_ff_ref, sum_attn_ref,
):
    incoming = summed(near, (far2, far1, far3))
    values = hidden[...]
    inverse = inverse_of(values)
    sum_ff_ref[...] = jnp.sum(incoming * values * inverse, axis=0, keepdims=True)
    grad_hidden = grad_result[...] + norm_back(values, inverse, gains[2:3, :], incoming)
    grad_hidden_ref[...] = grad_hidden
    values = branch[...]
    inverse = inverse_of(values)
    sum_attn_ref[...] = jnp.sum(grad_hidden * values * inverse, axis=0, keepdims=True)
    grad_ref[...] = norm_back(values, inverse, gains[1:2, :], grad_hidden).astype(BF)


def attention_back_kernel(
    ids, b0, b1, b2, b3, x, wq, wo, kv, pre_q, q, pre_k, k, v, shares, att, gain_q, gain_k,
    cosine, sine, gains, sum_attn_out, sum_ff_in, sum_ff_out,
    pair_own_ref, pair_sent_ref, sent_ref, kept_ref,
    grads, grad_kv, kv_part, part_a, part_b, pair_ref, sums,
):
    row = ids[0]
    scale = HEAD ** (-0.5)
    for j, block in enumerate((b0, b1, b2, b3)):
        grads[j * OWN : (j + 1) * OWN, :] = block[...]
    pair_ref[:, HEAD:] = dot(grads[...], att[...], 0, 0).astype(BF)
    grad_att = dot(grads[...], wo[...]).astype(BF)
    grad_shares = dot(grad_att, v[...], 1, 1)
    low = shares[...]
    wide = low.astype(F32)
    inner = jnp.sum(wide * grad_shares, axis=1, keepdims=True)
    grad_scores = (wide * (grad_shares - inner) * scale).astype(BF)
    turned = rotate(dot(grad_scores, k[...]), cosine[:QROWS, :], -sine[:QROWS, :])
    values = pre_q[...]
    inverse = inverse_of(values)
    sum_q = jnp.sum(turned * values * inverse, axis=0, keepdims=True)
    grad_q = norm_back(values, inverse, gain_q[...], turned).astype(BF)
    grad_kv[:, HEAD:] = dot(low, grad_att, 0, 0).astype(BF)
    turned = rotate(dot(grad_scores, q[...], 0, 0), cosine[...], -sine[...])
    values = pre_k[...].astype(F32)
    inverse = inverse_of(values)
    sum_k = jnp.sum(turned * values * inverse, axis=0, keepdims=True)
    grad_kv[:, :HEAD] = norm_back(values, inverse, gain_k[...], turned).astype(BF)

    back = dot(grad_kv[...], kv[...])
    back_q = back[:QROWS] + dot(grad_q, wq[...], 1, 1)
    sent_ref[:HEAD, :D] = back_q[:HEAD].astype(BF)
    sent_ref[HEAD:, :D] = back[QROWS : QROWS + HEAD].astype(BF)
    kept_ref[:HEAD, :D] = back_q[HEAD:].astype(BF)
    kept_ref[HEAD:, :D] = back[QROWS + HEAD :].astype(BF)

    part_q = dot(x[:QROWS, :], grad_q, 0, 0)
    pair_ref[:, :HEAD] = part_q.astype(BF)
    kv_part[...] = dot(grad_kv[...], x[...], 0, 0)
    weighted = (part_q * wq[...].astype(F32)).astype(BF)
    ones = jnp.ones((8, HEAD), BF)
    sum_in = dot(ones, weighted, 1, 1)[0:1, :] + jnp.sum(
        kv_part[...] * kv[...].astype(F32), axis=0, keepdims=True
    )
    sums[...] = jnp.zeros((128, 128), F32)
    place = 0
    for vector in (
        sum_in / gains[0:1, :], sum_attn_out[...], sum_ff_in[...], sum_ff_out[...], sum_q, sum_k
    ):
        for first in range(0, vector.shape[1], HALF):
            for begin in range(first, min(first + HALF, vector.shape[1]), 128):
                width = min(128, first + HALF - begin)
                sums[place : place + 1, :width] = vector[:, begin : begin + width]
                place += 1
    spare = sums[...].T[:, : BACK - WIDE].astype(BF)
    pair_own_ref[...] = pair_ref[pl.ds(pl.multiple_of(row * HALF, 64), HALF), :]
    pair_sent_ref[...] = pair_ref[pl.ds(pl.multiple_of((1 - row) * HALF, 64), HALF), :]

    @pl.when(row == 0)
    def _():
        part_a[...] = kv_part[:, :HALF].astype(BF)
        part_b[...] = kv_part[:, HALF:].astype(BF)

    @pl.when(row == 1)
    def _():
        part_a[...] = kv_part[:, HALF:].astype(BF)
        part_b[...] = kv_part[:, :HALF].astype(BF)

    for j in range(8):
        held = part_a if j < 4 else part_b
        target = sent_ref if j % 4 < 2 else kept_ref
        first = (j // 4) * 2 * OWN + (j % 2) * OWN
        at = pl.multiple_of(ids[4 + j] * 64, 64)
        target[first : first + 64, D:WIDE] = held[pl.ds(at, 64), :]
        target[first + 64 : first + 128, D:WIDE] = held[pl.ds(at + HEAD, 64), :]
        target[first : first + OWN, WIDE:] = spare


def end_kernel(
    ids, near, far2, far1, far3, residual, grad_hidden, gains,
    own_ref, sent_ref, kv_ref, turned,
):
    total = summed(near, (far2, far1, far3))
    kv_ref[...] = total[:, D:].astype(BF)
    values = residual[...]
    back = norm_back(values, inverse_of(values), gains[0:1, :], total[:, :D])
    turned[...] = (grad_hidden[...] + back).T
    split_halves(ids[0], turned, own_ref, sent_ref)


def join_strips_kernel(ids, own, one, two, three, out_ref):
    join_strips(ids[3], own, one, two, three, out_ref)


def join_strips(at, own, one, two, three, out_ref):
    for step, piece in ((0, own), (1, one), (2, two), (3, three)):
        j = (at + 4 - step) % 4
        out_ref[:, pl.ds(pl.multiple_of(j * STRIDE, 128), STRIDE)] = piece[:, :STRIDE]

        @pl.when(j == 3)
        def _():
            out_ref[:, 4 * STRIDE : THREE] = piece[:, STRIDE:PIECE]


def widen_kernel(at, own, one, two, three, out_ref):
    join_strips(at[0], own, one, two, three, out_ref)
    terms = [piece[:, PIECE:].astype(F32) for piece in (own, one, two, three)]
    out_ref[:, THREE:] = ((terms[0] + terms[2]) + (terms[1] + terms[3])).astype(BF)


def results_kernel(
    ids, o0, o1, o3, o_low, o_high, p0, p1, p3, p_low, p_high,
    gate_ref, up_ref, down_ref, query_ref, out_ref, key_ref, value_ref, sums_ref, across, kv,
):
    half = LOAD // 2
    for low, high, first in ((o_low, o_high, True), (p_low, p_high, False)):
        across[:, :half] = low[...]
        across[:, half:] = high[...]
        pieces = ((0, o0), (1, o1), (3, o3)) if first else ((0, p0), (1, p1), (3, p3))
        for step, piece in pieces + ((2, across),):
            place = ((ids[2] if first else ids[3]) + 4 - step) % 4
            rows = pl.ds(pl.multiple_of(place * CHUNK, 16), CHUNK)
            for row in range(2):

                @pl.when(ids[0] == row)
                def _():
                    block = row if first else 1 - row
                    width = UNITS if block == 0 else HIDDEN - UNITS
                    for m, target in enumerate((gate_ref, up_ref, down_ref)):
                        target[rows, block * UNITS : block * UNITS + width] = piece[
                            :, m * UNITS : m * UNITS + width
                        ].astype(F32)

            if first:
                out_ref[rows, :] = piece[:, THREE : THREE + HEAD].astype(F32)

                @pl.when(place == 0)
                def _():
                    sums = piece[:64, THREE + HEAD :].astype(F32)
                    for v in range(4):
                        sums_ref[8 * v : 8 * v + 5, :] = jnp.where(
                            ids[0] == 0, sums[10 * v : 10 * v + 5], sums[10 * v + 5 : 10 * v + 10]
                        )
                    sums_ref[32:36, :] = sums[40:44]
            else:
                query_ref[rows, :] = piece[:, THREE : THREE + HEAD].astype(F32)
                kv[rows, :] = piece[:, THREE + HEAD :].astype(F32)
    turned = kv[...].T
    key_ref[...] = turned[:64]
    value_ref[...] = turned[64:]


def cross_kernel(ids, kept, got, near_ref, *refs):
    near_ref[...] = kept[:OWN, :].astype(F32) + got[:OWN, :].astype(F32)
    for i, target in enumerate(refs):
        rows = slice((i + 1) * OWN, (i + 2) * OWN)
        target[...] = (kept[rows, :].astype(F32) + got[rows, :].astype(F32)).astype(BF)


def gather_blocks(own, ready=None):
    far1, far3 = move_z(own, 1), move_z(own, 3)
    near = move_core(own)
    far2 = move_z(own, 2)
    held = [far2, far1, far3]
    if ready is not None:
        held, _ = lax.optimization_barrier((held, ready))
    return [own] + held, [near] + [move_core(block) for block in held]


def reduce_blocks(ids, sent, kept, steps=(2, 3, 1)):
    width = kept.shape[1]
    got = move_core(sent)
    near, *crossed = call(
        cross_kernel,
        [shape(OWN, width, F32)] + [shape(OWN, width, BF)] * len(steps),
        ids,
        [kept, got],
    )
    return [near] + [move_z(block, step) for block, step in zip(crossed, steps)], crossed


def ring_gather(band, axis, low_width, ready=None):
    one, three = move_plane(band, axis, 1), move_plane(band, axis, 3)
    if ready is not None:
        (one, three), _ = lax.optimization_barrier(((one, three), ready))
    low = move_plane(one[:, :low_width], axis, 1)
    high = move_plane(three[:, low_width:], axis, 3)
    return [band, one, three, low, high]


def layout(lengths_row, places):
    slots = lengths_row.shape[0]
    order = jnp.arange(slots, dtype=jnp.int32)
    ends = jnp.sum(jnp.where(order[None, :] <= order[:, None], lengths_row[None, :], 0), axis=1)
    passed = places[:, None] >= ends[None, :]
    sequence = jnp.sum(passed.astype(jnp.int32), axis=1)
    start_of = jnp.max(jnp.where(passed, ends[None, :], 0), axis=1)
    return (sequence, places - start_of, (places < ends[slots - 1]).astype(F32))


def body(
    tokens, doc_lengths, w_query, w_key, w_value, w_out, w_gate, w_up, w_down,
    gain_attn_in, gain_attn_out, gain_ff_in, gain_ff_out, gain_query, gain_key, cotangent,
):
    row = lax.axis_index("row")
    col = lax.axis_index("col")
    plane = lax.axis_index("dp")
    x_at, y_at = plane // 4, plane % 4
    near_pair, far_pair = col ^ (2 * (1 - row)), col ^ (2 * row)
    owner_cols = [col ^ 1, col ^ 3, col, col ^ 2, near_pair ^ 1, far_pair ^ 1, near_pair, far_pair]
    ids = jnp.stack([row, col, x_at, y_at] + owner_cols).astype(jnp.int32)

    def exchange_rows(block):
        turned = block.T
        own = lax.dynamic_slice_in_dim(turned, row * OWN, OWN, 1)
        return own, move_row(lax.dynamic_slice_in_dim(turned, (1 - row) * OWN, OWN, 1))

    def join_rows(own, got):
        got = got.astype(own.dtype)
        return jnp.where(
            row == 0, jnp.concatenate([own, got], axis=1), jnp.concatenate([got, own], axis=1)
        ).T

    tokens_own, tokens_other = exchange_rows(tokens)
    starts = jnp.stack(
        [
            owner_cols[j] * 256 + (row if j < 4 else 1 - row) * OWN
            for j in range(8)
        ]
    )
    places = (starts[:, None] + jnp.arange(OWN, dtype=jnp.int32)[None, :]).reshape(-1)
    sequence, positions, live = layout(doc_lengths[0], places)
    live_own = live[HEAD : HEAD + OWN][:, None]
    frequency = ROPE_BASE ** (-2.0 * jnp.arange(HEAD // 2, dtype=F32) / HEAD)
    angles = positions.astype(F32)[:, None] * frequency
    cosine, sine = jnp.cos(angles), jnp.sin(angles)
    gain_q, gain_k = gain_query[None], gain_key[None]

    gain_flat = jnp.concatenate([gain_attn_in, gain_attn_out, gain_ff_in, gain_ff_out])
    gain_own, gain_other = gain_flat.reshape(4, HALF), move_row(gain_flat).reshape(4, HALF)
    gains = jnp.where(
        row == 0,
        jnp.concatenate([gain_own, gain_other], axis=1),
        jnp.concatenate([gain_other, gain_own], axis=1),
    )

    down_turned = w_down.T
    (piece,) = call(
        piece_kernel,
        [shape(CHUNK, PIECE, BF)],
        ids,
        [w_gate, w_up, down_turned],
        [
            pltpu.VMEM((3, CHUNK, HIDDEN), BF), pltpu.VMEM((CHUNK, THREE), BF),
            pltpu.SemaphoreType.DMA((3,)),
        ],
        limit=24,
        after=(tokens_other,),
        raw=True,
        us=2,
    )
    query_other = move_row(w_query)
    kv_own = jnp.concatenate([w_key.T, w_value.T], axis=0)
    residual, payload = call(
        begin_kernel,
        [shape(OWN, D, F32), shape(OWN, WIDE, BF)],
        ids,
        [tokens_own, tokens_other, gains, kv_own],
        after=(query_other, piece),
        us=2,
    )
    mine, swapped = gather_blocks(payload)
    out_own, _ = lax.optimization_barrier((w_out.T, mine[1]))
    out_other = move_row(out_own)

    (
        normed_in, query_weights, kv_weights, pre_query, queries, pre_key, keys, values, shares,
        attended,
    ) = call(
        attention_kernel,
        [
            shape(KEYS, D, BF), shape(D, HEAD, BF), shape(2 * HEAD, D, BF),
            shape(QROWS, HEAD, F32), shape(QROWS, HEAD, BF), shape(KEYS, HEAD, BF),
            shape(KEYS, HEAD, BF), shape(KEYS, HEAD, BF), shape(QROWS, KEYS, BF),
            shape(QROWS, HEAD, BF),
        ],
        ids,
        [
            swapped[0], swapped[1], mine[0], mine[1], swapped[2], swapped[3], mine[2], mine[3],
            w_query, query_other, gain_q, gain_k, cosine, sine,
            sequence[:QROWS, None], positions[:QROWS, None], sequence[None], positions[None],
        ],
        [pltpu.VMEM((2 * HEAD, HALF), BF)] * 2,
        limit=24,
        us=10,
    )
    cot_own, cot_other = exchange_rows(cotangent)
    out_weights, sent, kept = call(
        out_kernel,
        [shape(D, HEAD, BF), shape(HEAD, D, BF), shape(HEAD, D, F32)],
        ids,
        [attended, out_own, out_other],
        us=2,
    )
    reduced, _ = reduce_blocks(ids, sent, kept, (2,))
    branch_attn, hidden_mid, normed_ff = call(
        middle_kernel,
        [shape(OWN, D, F32), shape(OWN, D, F32), shape(OWN, D, BF)],
        ids,
        reduced + [residual, gains],
    )

    moved, _ = lax.optimization_barrier((move_row(piece), attended))
    strips = [moved] + [move_plane(moved, "y", step) for step in (1, 2, 3)]
    (band,) = call(join_strips_kernel, [shape(CHUNK, THREE, BF)], ids, strips)
    weight_bands = ring_gather(band, "x", LOW, normed_ff)
    ff_weights = call(
        weights_kernel, [shape(D, UNITS, BF)] * 3, ids,
        [w_gate, w_up, down_turned] + weight_bands,
        [pltpu.VMEM((CHUNK, THREE), BF)],
        limit=24,
        us=4,
    )
    mine, swapped = gather_blocks(normed_ff, ff_weights[0])
    ff_in, activated, by_up, by_gate, sent, kept = call(
        forward_kernel,
        [shape(KEYS, D, BF)]
        + [shape(KEYS, UNITS, BF)] * 3
        + [shape(512, D, BF)] * 2,
        ids,
        swapped + mine + list(ff_weights),
        limit=24,
        us=14,
    )
    mixed_own, mixed_sent, grad_branch_ff, grad_result, sum_ff_out = call(
        turn_kernel,
        [
            shape(HALF, OWN, BF), shape(HALF, OWN, BF), shape(OWN, D, BF),
            shape(OWN, D, F32), shape(1, D, F32),
        ],
        ids,
        reduce_blocks(ids, sent, kept)[0] + [hidden_mid, cot_own, cot_other, live_own, gains],
        [pltpu.VMEM((D, OWN), F32)],
        us=3,
    )
    mine, swapped = gather_blocks(grad_branch_ff)
    ff_grad, grad_gate, grad_up, sent, kept = call(
        backward_kernel,
        [shape(KEYS, D, BF)] + [shape(KEYS, UNITS, BF)] * 2 + [shape(512, D, BF)] * 2,
        ids,
        swapped + mine + [by_up, by_gate] + list(ff_weights),
        limit=24,
        us=10,
    )
    reduced, crossed = reduce_blocks(ids, sent, kept)
    bands = call(
        products_kernel,
        (
            [shape(CHUNK, THREE, BF)] * 3
            + [shape(CHUNK, LOW, BF), shape(CHUNK, THREE - LOW, BF)]
        )
        * 2,
        ids,
        [ff_in, ff_grad, activated, grad_gate, grad_up],
        [pltpu.VMEM((D, THREE), BF)],
        limit=24,
        us=9,
        after=(crossed[0],),
    )
    grad_hidden, grad_branch_attn, sum_ff_in, sum_attn_out = call(
        return_kernel,
        [shape(OWN, D, F32), shape(OWN, D, BF), shape(1, D, F32), shape(1, D, F32)],
        ids,
        reduced + [hidden_mid, branch_attn, grad_result, gains],
        after=(bands[0],),
    )
    far = move_z(grad_branch_attn, 2)
    near, far_near = move_core(grad_branch_attn), move_core(far)
    def begin_ring(pieces, axis):
        band0, band1, band3, low, high = pieces
        one, three = call(
            join_kernel,
            [shape(CHUNK, THREE, BF)] * 2,
            ids,
            [band1, band3, move_plane(low, axis, 1), move_plane(high, axis, 3)],
        )
        return band0, move_plane(one, axis, 1), move_plane(three, axis, 3)

    own_ring, other_ring = begin_ring(bands[:5], "x"), begin_ring(bands[5:], "y")
    pair_kept, pair_sent, sent, kept = call(
        attention_back_kernel,
        [
            shape(HALF, 2 * HEAD, BF), shape(HALF, 2 * HEAD, BF), shape(512, BACK, BF),
            shape(512, BACK, BF),
        ],
        ids,
        [near, far_near, grad_branch_attn, far]
        + [
            a
            for a in (
                normed_in, query_weights, out_weights, kv_weights, pre_query, queries, pre_key, keys, values,
                shares, attended,
            )
        ]
        + [
            gain_q, gain_k, cosine, sine, gains, sum_attn_out, sum_ff_in, sum_ff_out,
        ],
        [
            pltpu.VMEM((QROWS, D), BF), pltpu.VMEM((KEYS, 2 * HEAD), BF),
            pltpu.VMEM((2 * HEAD, D), F32), pltpu.VMEM((2 * HEAD, HALF), BF),
            pltpu.VMEM((2 * HEAD, HALF), BF), pltpu.VMEM((D, 2 * HEAD), BF),
            pltpu.VMEM((128, 128), F32),
        ],
        limit=24,
        us=9,
        after=(own_ring[1], own_ring[2], other_ring[1], other_ring[2]),
    )
    pair_got = move_row(pair_sent)
    reduced, crossed = reduce_blocks(ids, sent, kept)
    tokens_grad_own, tokens_grad_sent, kv_sum = call(
        end_kernel,
        [shape(HALF, OWN, F32), shape(HALF, OWN, BF), shape(OWN, BACK - D, BF)],
        ids,
        reduced + [residual, grad_hidden, gains],
        [pltpu.VMEM((D, OWN), F32)],
    )
    mixed_got, tokens_got = move_row(mixed_sent), move_row(tokens_grad_sent)
    mixed = join_rows(mixed_own, mixed_got)
    grad_tokens = join_rows(tokens_grad_own, tokens_got)

    def reduce_two(ring, axis, second, first):
        band0, one, three = ring
        strips = call(
            functools.partial(fold_kernel, first),
            [shape(CHUNK, PIECE + EXTRA, BF)] * 4,
            ids,
            [
                band0, one, three, pair_kept, pair_got, kv_sum,
            ],
            [pltpu.VMEM((CHUNK, THREE), BF), pltpu.VMEM((HALF, EXTRA), BF)],
        )
        total = strips[0].astype(F32)
        for step in (1, 3, 2):
            total = total + move_plane(strips[step], second, step).astype(F32)
        return total.astype(BF)

    def gather_two(held, axis, second, second_at):
        strips = [held] + [move_plane(held, second, step) for step in (1, 2, 3)]
        (band,) = call(
            widen_kernel, [shape(CHUNK, LOAD, BF)], second_at[None], strips,
            after=(mixed_got, tokens_got),
        )
        return ring_gather(band, axis, LOAD // 2)

    own_total = reduce_two(own_ring, "x", "y", True)
    other_total = reduce_two(other_ring, "y", "x", False)
    peer_piece = move_row(other_total[:, :PIECE])
    own_held = jnp.concatenate([own_total[:, :PIECE], other_total[:, PIECE:]], axis=1)
    peer_held = jnp.concatenate([peer_piece, own_total[:, PIECE:]], axis=1)
    own_bands = gather_two(own_held, "x", "y", y_at)
    peer_bands = gather_two(peer_held, "y", "x", x_at)
    grad_w_gate, grad_w_up, grad_w_down, grad_w_query, grad_w_out, grad_key_w, grad_value_w, sums = call(
        results_kernel,
        [shape(HALF, HIDDEN, F32)] * 3
        + [shape(HALF, HEAD, F32)] * 2
        + [shape(64, HALF, F32)] * 2
        + [shape(40, 128, F32)],
        ids,
        own_bands + peer_bands,
        [pltpu.VMEM((CHUNK, LOAD), BF), pltpu.VMEM((HALF, 128), F32)],
        limit=24,
        after=(mixed, grad_tokens),
        us=7,
    )

    def gain_part(i):
        return sums[8 * i : 8 * i + 5].reshape(-1)[:HALF]

    return (
        mixed,
        grad_tokens,
        grad_w_query,
        grad_key_w.T,
        grad_value_w.T,
        grad_w_out.T,
        grad_w_gate,
        grad_w_up,
        grad_w_down.T,
        gain_part(0),
        gain_part(1),
        gain_part(2),
        gain_part(3),
        sums[32:34].reshape(-1),
        sums[34:36].reshape(-1),
    )


def solution(mesh):
    return jax.shard_map(
        body,
        mesh=mesh,
        in_specs=(
            P(("dp", "col"), "row"),
            P("dp", None),
            P("row", "col"),
            P("row", "col"),
            P("row", "col"),
            P("col", "row"),
            P("row", "col"),
            P("row", "col"),
            P("col", "row"),
            P("row"),
            P("row"),
            P("row"),
            P("row"),
            P(),
            P(),
            P(("dp", "col"), "row"),
        ),
        out_specs=(
            P(("dp", "col"), "row"),
            P(("dp", "col"), "row"),
            P("row", "col"),
            P("row", "col"),
            P("row", "col"),
            P("col", "row"),
            P("row", "col"),
            P("row", "col"),
            P("col", "row"),
            P("row"),
            P("row"),
            P("row"),
            P("row"),
            P(),
            P(),
        ),
        check_vma=False,
    )
```

```python
import functools

import jax
import jax.numpy as jnp
from jax import lax
from jax.experimental import pallas as pl
from jax.experimental.pallas import tpu as pltpu
from jax.sharding import PartitionSpec as P

WINDOW = 512
EPSILON = 1e-06
ROPE_BASE = 10000.0
MASKED = -1e30
GROUP = ("row", "col")
BF = jnp.bfloat16
F32 = jnp.float32
OWN = 128
D = 1152
HALF = 576
HIDDEN = 1728
UNITS = 896
THREE = 3 * UNITS
HEAD = 256
QROWS = 512
KEYS = 1024
WIDE = D + HALF
BACK = WIDE + 64
CHUNK = 144
PIECE = 768
STRIDE = 640
LOW = 1280
EXTRA = 3 * 128
LOAD = THREE + EXTRA
GELU_C = 0.7978845608028654
GELU_A = 0.044715


def member(z, core):
    return (z % 2) * 4 + (z // 2) * 2 + core


def z_pairs(step):
    return [(member(z, c), member((z + step) % 4, c)) for z in range(4) for c in range(2)]


CORE_PAIRS = [(member(z, c), member(z, 1 - c)) for z in range(4) for c in range(2)]
ROW_PAIRS = [(0, 1), (1, 0)]


def move_z(values, step):
    return lax.ppermute(values, GROUP, z_pairs(step % 4))


def move_core(values):
    return lax.ppermute(values, GROUP, CORE_PAIRS)


def move_row(values):
    return lax.ppermute(values, "row", ROW_PAIRS)


def move_plane(values, axis, step):
    if axis == "x":
        pairs = [(x * 4 + y, ((x + step) % 4) * 4 + y) for x in range(4) for y in range(4)]
    else:
        pairs = [(x * 4 + y, x * 4 + (y + step) % 4) for x in range(4) for y in range(4)]
    return lax.ppermute(values, "dp", pairs)


def dot(left, right, left_dim=1, right_dim=0):
    return lax.dot_general(
        left, right, (((left_dim,), (right_dim,)), ((), ())), preferred_element_type=F32
    )


def shape(rows, width, dtype):
    return jax.ShapeDtypeStruct((rows, width), dtype)


def call(kernel, outs, ids, args, scratch=(), limit=16, after=(), raw=False, us=1):
    def run(ids_ref, *refs):
        kernel(ids_ref, *refs[len(after) :])

    return pl.pallas_call(
        run,
        out_shape=tuple(outs),
        in_specs=[pl.BlockSpec(memory_space=pltpu.SMEM)]
        + [pl.BlockSpec(memory_space=pl.ANY)] * len(after)
        + [pl.BlockSpec(memory_space=pl.ANY if raw else pltpu.VMEM)] * len(args),
        out_specs=tuple(pl.BlockSpec(memory_space=pltpu.VMEM) for _ in outs),
        scratch_shapes=list(scratch),
        compiler_params=pltpu.CompilerParams(vmem_limit_bytes=limit * 1024 * 1024),
        cost_estimate=pl.CostEstimate(
            flops=int(us * 1.15e9), bytes_accessed=1024, transcendentals=0
        ),
    )(ids, *after, *args)


def inverse_of(values):
    return lax.rsqrt(jnp.mean(values * values, axis=1, keepdims=True) + EPSILON)


def norm_back(values, inverse, gain, incoming):
    inner = jnp.mean(incoming * gain * values, axis=1, keepdims=True)
    return inverse * gain * incoming - values * (inverse * inverse * inverse * inner)


def rotate(values, cosine, sine):
    half = values.shape[1] // 2
    first, second = values[:, :half], values[:, half:]
    return jnp.concatenate(
        [first * cosine - second * sine, second * cosine + first * sine], axis=1
    )


def own_rows(row, own_ref, other_ref):
    own = own_ref[...].astype(F32)
    other = other_ref[...].astype(F32)
    first = jnp.where(row == 0, own, other)
    second = jnp.where(row == 0, other, own)
    return jnp.concatenate([first, second], axis=0).T


def split_halves(row, turned_ref, own_ref, sent_ref):
    own_ref[...] = turned_ref[pl.ds(pl.multiple_of(row * HALF, 64), HALF), :].astype(own_ref.dtype)
    sent_ref[...] = turned_ref[pl.ds(pl.multiple_of((1 - row) * HALF, 64), HALF), :].astype(
        sent_ref.dtype
    )


def summed(near, far):
    total = near[...]
    for piece in far:
        total = total + piece[...].astype(F32)
    return total


def piece_kernel(ids, gate, up, down, out_ref, bands, strip, sems):
    copies = []
    for m, source in enumerate((gate, up, down)):
        rows = pl.ds(pl.multiple_of(ids[2] * CHUNK, 16), CHUNK)
        copies.append(pltpu.make_async_copy(source.at[rows, :], bands.at[m], sems.at[m]))
    for copy in copies:
        copy.start()
    for copy in copies:
        copy.wait()
    for row in range(2):

        @pl.when(ids[0] == row)
        def _():
            for m in range(3):
                if row == 0:
                    end = m * UNITS + HIDDEN - UNITS
                    strip[:, m * UNITS : end] = bands[m, :, UNITS:]
                    strip[:, end : (m + 1) * UNITS] = jnp.zeros((CHUNK, 2 * UNITS - HIDDEN), BF)
                else:
                    strip[:, m * UNITS : (m + 1) * UNITS] = bands[m, :, :UNITS]

    out_ref[...] = strip[:, pl.ds(pl.multiple_of(ids[3] * STRIDE, 128), PIECE)]


def begin_kernel(ids, own, other, gains, kv, residual_ref, payload_ref):
    values = own_rows(ids[0], own, other)
    residual_ref[...] = values
    payload_ref[:, :D] = (values * inverse_of(values) * gains[0:1, :]).astype(BF)
    payload_ref[:, D:] = kv[...]


def weights_kernel(
    ids, gate, up, down, own, one, three, low, high, gate_ref, up_ref, down_ref, across
):
    sources, targets = (gate, up, down), (gate_ref, up_ref, down_ref)
    across[:, :LOW] = low[...]
    across[:, LOW:] = high[...]
    for row in range(2):

        @pl.when(ids[0] == row)
        def _():
            mine = slice(row * HALF, (row + 1) * HALF)
            for source, target in zip(sources, targets):
                if row == 0:
                    target[mine, :] = source[:, :UNITS]
                else:
                    target[mine, : HIDDEN - UNITS] = source[:, UNITS:]
                    target[mine, HIDDEN - UNITS :] = jnp.zeros((HALF, 2 * UNITS - HIDDEN), BF)

    for step, band in ((0, own), (1, one), (2, across), (3, three)):
        place = (ids[2] + 4 - step) % 4
        rows = pl.ds(pl.multiple_of((1 - ids[0]) * HALF + place * CHUNK, 16), CHUNK)
        for m, target in enumerate(targets):
            target[rows, :] = band[:, m * UNITS : (m + 1) * UNITS]


def attention_kernel(
    ids, b0, b1, b2, b3, b4, b5, b6, b7, query_own, query_other, gain_q, gain_k, cosine, sine,
    seq_q, pos_q, seq_k, pos_k,
    x_ref, wq_ref, kv_ref, pre_q_ref, q_ref, pre_k_ref, k_ref, v_ref, shares_ref, att_ref,
    part_a, part_b,
):
    row = ids[0]
    blocks = (b0, b1, b2, b3, b4, b5, b6, b7)
    for j, block in enumerate(blocks):
        x_ref[j * OWN : (j + 1) * OWN, :] = block[:, :D]
        held = part_a if j < 4 else part_b
        at = pl.multiple_of(ids[4 + j] * 64, 64)
        held[pl.ds(at, 64), :] = block[:64, D:]
        held[pl.ds(at + HEAD, 64), :] = block[64:, D:]
    wq_ref[pl.ds(pl.multiple_of(row * HALF, 64), HALF), :] = query_own[...]
    wq_ref[pl.ds(pl.multiple_of((1 - row) * HALF, 64), HALF), :] = query_other[...]

    @pl.when(row == 0)
    def _():
        kv_ref[:, :HALF] = part_a[...]
        kv_ref[:, HALF:] = part_b[...]

    @pl.when(row == 1)
    def _():
        kv_ref[:, :HALF] = part_b[...]
        kv_ref[:, HALF:] = part_a[...]

    x = x_ref[...]
    pre_q = dot(x[:QROWS], wq_ref[...])
    pre_q_ref[...] = pre_q
    queries = rotate(
        pre_q * inverse_of(pre_q) * gain_q[...], cosine[:QROWS, :], sine[:QROWS, :]
    ).astype(BF)
    q_ref[...] = queries
    pre_k = dot(x, kv_ref[:HEAD, :], 1, 1).astype(BF)
    pre_k_ref[...] = pre_k
    values = dot(x, kv_ref[HEAD:, :], 1, 1).astype(BF)
    v_ref[...] = values
    pre_k = pre_k.astype(F32)
    keys = rotate(pre_k * inverse_of(pre_k) * gain_k[...], cosine[...], sine[...]).astype(BF)
    k_ref[...] = keys
    distance = pos_q[...] - pos_k[...]
    allowed = (seq_q[...] == seq_k[...]) & (distance >= 0) & (distance < WINDOW)
    scores = jnp.where(allowed, dot(queries, keys, 1, 1) * (HEAD ** (-0.5)), MASKED)
    weights = jnp.exp(scores - jnp.max(scores, axis=1, keepdims=True))
    shares = (weights / jnp.sum(weights, axis=1, keepdims=True)).astype(BF)
    shares_ref[...] = shares
    attended = dot(shares, values).astype(BF)
    att_ref[...] = attended


def out_kernel(ids, attended, out_own, out_other, wo_ref, sent_ref, kept_ref):
    row = ids[0]
    wo_ref[pl.ds(pl.multiple_of(row * HALF, 64), HALF), :] = out_own[...]
    wo_ref[pl.ds(pl.multiple_of((1 - row) * HALF, 64), HALF), :] = out_other[...]
    partial = dot(attended[...], wo_ref[...], 1, 1)
    sent_ref[...] = partial[:HEAD].astype(BF)
    kept_ref[...] = partial[HEAD:]


def middle_kernel(ids, near, far, residual, gains, branch_ref, hidden_ref, normed_ref):
    branch = summed(near, (far,))
    branch_ref[...] = branch
    hidden = residual[...] + branch * inverse_of(branch) * gains[1:2, :]
    hidden_ref[...] = hidden
    normed_ref[...] = (hidden * inverse_of(hidden) * gains[2:3, :]).astype(BF)


def forward_kernel(
    ids, b0, b1, b2, b3, b4, b5, b6, b7, w_gate, w_up, w_down,
    x_ref, act_ref, by_up_ref, by_gate_ref, sent_ref, kept_ref,
):
    for j, block in enumerate((b0, b1, b2, b3, b4, b5, b6, b7)):
        x_ref[j * OWN : (j + 1) * OWN, :] = block[...]

    @pl.loop(0, 2)
    def _(i):
        rows = pl.ds(pl.multiple_of(i * 512, 512), 512)
        x = x_ref[rows, :]
        partial = None
        for low, high in ((0, 256), (256, 512), (512, UNITS)):
            columns = slice(low, high)
            gate = dot(x, w_gate[:, columns])
            up = dot(x, w_up[:, columns])
            square = gate * gate
            bend = jnp.tanh(gate * (GELU_C + GELU_C * GELU_A * square))
            ramp = 0.5 + 0.5 * bend
            soft = gate * ramp
            slope = ramp + soft * (1.0 - bend) * (GELU_C + 3.0 * GELU_C * GELU_A * square)
            act = (soft * up).astype(BF)
            act_ref[rows, columns] = act
            by_up_ref[rows, columns] = soft.astype(BF)
            by_gate_ref[rows, columns] = (up * slope).astype(BF)
            product = dot(act, w_down[:, columns], 1, 1)
            partial = product if partial is None else partial + product
        partial = partial.astype(BF)

        @pl.when(i == 0)
        def _():
            sent_ref[...] = partial

        @pl.when(i == 1)
        def _():
            kept_ref[...] = partial


def turn_kernel(
    ids, near, far2, far1, far3, hidden, cot_own, cot_other, live, gains,
    mixed_own_ref, mixed_sent_ref, grad_ref, result_ref, sum_ref, turned,
):
    row = ids[0]
    branch = summed(near, (far2, far1, far3))
    inverse = inverse_of(branch)
    turned[...] = (hidden[...] + branch * inverse * gains[3:4, :]).T
    split_halves(row, turned, mixed_own_ref, mixed_sent_ref)
    grad_result = own_rows(row, cot_own, cot_other) * live[...]
    result_ref[...] = grad_result
    sum_ref[...] = jnp.sum(grad_result * branch * inverse, axis=0, keepdims=True)
    grad_ref[...] = norm_back(branch, inverse, gains[3:4, :], grad_result).astype(BF)


def backward_kernel(
    ids, b0, b1, b2, b3, b4, b5, b6, b7, by_up, by_gate, w_gate, w_up, w_down,
    g_ref, grad_gate_ref, grad_up_ref, sent_ref, kept_ref,
):
    for j, block in enumerate((b0, b1, b2, b3, b4, b5, b6, b7)):
        g_ref[j * OWN : (j + 1) * OWN, :] = block[...]

    @pl.loop(0, 2)
    def _(i):
        rows = pl.ds(pl.multiple_of(i * 512, 512), 512)
        grad = dot(g_ref[rows, :], w_down[...])
        grad_gate = (grad * by_gate[rows, :].astype(F32)).astype(BF)
        grad_up = (grad * by_up[rows, :].astype(F32)).astype(BF)
        grad_gate_ref[rows, :] = grad_gate
        grad_up_ref[rows, :] = grad_up
        partial = (dot(grad_gate, w_gate[...], 1, 1) + dot(grad_up, w_up[...], 1, 1)).astype(BF)

        @pl.when(i == 0)
        def _():
            sent_ref[...] = partial

        @pl.when(i == 1)
        def _():
            kept_ref[...] = partial


def products_kernel(ids, x, grads, act, grad_gate, grad_up, *refs):
    bands, whole = refs[:10], refs[10]

    @pl.loop(0, 3)
    def _(i):
        rows = pl.ds(pl.multiple_of(i * 384, 384), 384)
        part = x[:, rows]
        whole[rows, :UNITS] = dot(part, grad_gate[...], 0, 0).astype(BF)
        whole[rows, UNITS : 2 * UNITS] = dot(part, grad_up[...], 0, 0).astype(BF)
        whole[rows, 2 * UNITS :] = dot(grads[:, rows], act[...], 0, 0).astype(BF)

    for i in range(8):
        half = ids[0] if i < 4 else 1 - ids[0]
        place = ((ids[2] if i < 4 else ids[3]) + i) % 4
        rows = pl.ds(pl.multiple_of(half * HALF + place * CHUNK, 16), CHUNK)
        at = (i // 4) * 5
        if i % 4 == 2:
            bands[at + 3][...] = whole[rows, :LOW]
            bands[at + 4][...] = whole[rows, LOW:]
        else:
            bands[at + min(i % 4, 2)][...] = whole[rows, :]


def join_kernel(ids, band1, band3, low, high, one_ref, three_ref):
    one_ref[:, :LOW] = (band1[:, :LOW].astype(F32) + low[...].astype(F32)).astype(BF)
    one_ref[:, LOW:] = band1[:, LOW:]
    three_ref[:, :LOW] = band3[:, :LOW]
    three_ref[:, LOW:] = (band3[:, LOW:].astype(F32) + high[...].astype(F32)).astype(BF)


def fold_kernel(first, ids, own, one, three, pair_own, pair_got, kv, s0, s1, s2, s3, folded, extra):
    total = own[...].astype(F32) + one[...].astype(F32)
    folded[...] = (total + three[...].astype(F32)).astype(BF)
    columns = slice(0, HEAD) if first else slice(HEAD, 2 * HEAD)
    extra[:, :HEAD] = (pair_own[:, columns].astype(F32) + pair_got[:, columns].astype(F32)).astype(
        BF
    )
    turned = kv[...].astype(F32).T
    if first:
        extra[:, HEAD:] = turned[:HALF].astype(BF)
    else:
        extra[:64, HEAD:] = turned[HALF:].astype(BF)
        extra[64:, HEAD:] = jnp.zeros((HALF - 64, 128), BF)
    at = ids[3] if first else ids[2]
    for step, strip in enumerate((s0, s1, s2, s3)):
        place = (at + step) % 4
        strip[:, :PIECE] = folded[:, pl.ds(pl.multiple_of(place * STRIDE, 128), PIECE)]
        strip[:, PIECE:] = extra[pl.ds(pl.multiple_of(place * CHUNK, 16), CHUNK), :]


def return_kernel(
    ids, near, far2, far1, far3, hidden, branch, grad_result, gains,
    grad_hidden_ref, grad_ref, sum_ff_ref, sum_attn_ref,
):
    incoming = summed(near, (far2, far1, far3))
    values = hidden[...]
    inverse = inverse_of(values)
    sum_ff_ref[...] = jnp.sum(incoming * values * inverse, axis=0, keepdims=True)
    grad_hidden = grad_result[...] + norm_back(values, inverse, gains[2:3, :], incoming)
    grad_hidden_ref[...] = grad_hidden
    values = branch[...]
    inverse = inverse_of(values)
    sum_attn_ref[...] = jnp.sum(grad_hidden * values * inverse, axis=0, keepdims=True)
    grad_ref[...] = norm_back(values, inverse, gains[1:2, :], grad_hidden).astype(BF)


def attention_back_kernel(
    ids, b0, b1, b2, b3, x, wq, wo, kv, pre_q, q, pre_k, k, v, shares, att, gain_q, gain_k,
    cosine, sine, gains, sum_attn_out, sum_ff_in, sum_ff_out,
    pair_own_ref, pair_sent_ref, sent_ref, kept_ref,
    grads, grad_kv, kv_part, part_a, part_b, pair_ref, sums,
):
    row = ids[0]
    scale = HEAD ** (-0.5)
    for j, block in enumerate((b0, b1, b2, b3)):
        grads[j * OWN : (j + 1) * OWN, :] = block[...]
    pair_ref[:, HEAD:] = dot(grads[...], att[...], 0, 0).astype(BF)
    grad_att = dot(grads[...], wo[...]).astype(BF)
    grad_shares = dot(grad_att, v[...], 1, 1)
    low = shares[...]
    wide = low.astype(F32)
    inner = jnp.sum(wide * grad_shares, axis=1, keepdims=True)
    grad_scores = (wide * (grad_shares - inner) * scale).astype(BF)
    turned = rotate(dot(grad_scores, k[...]), cosine[:QROWS, :], -sine[:QROWS, :])
    values = pre_q[...]
    inverse = inverse_of(values)
    sum_q = jnp.sum(turned * values * inverse, axis=0, keepdims=True)
    grad_q = norm_back(values, inverse, gain_q[...], turned).astype(BF)
    grad_kv[:, HEAD:] = dot(low, grad_att, 0, 0).astype(BF)
    turned = rotate(dot(grad_scores, q[...], 0, 0), cosine[...], -sine[...])
    values = pre_k[...].astype(F32)
    inverse = inverse_of(values)
    sum_k = jnp.sum(turned * values * inverse, axis=0, keepdims=True)
    grad_kv[:, :HEAD] = norm_back(values, inverse, gain_k[...], turned).astype(BF)

    back = dot(grad_kv[...], kv[...])
    back_q = back[:QROWS] + dot(grad_q, wq[...], 1, 1)
    sent_ref[:HEAD, :D] = back_q[:HEAD].astype(BF)
    sent_ref[HEAD:, :D] = back[QROWS : QROWS + HEAD].astype(BF)
    kept_ref[:HEAD, :D] = back_q[HEAD:].astype(BF)
    kept_ref[HEAD:, :D] = back[QROWS + HEAD :].astype(BF)

    part_q = dot(x[:QROWS, :], grad_q, 0, 0)
    pair_ref[:, :HEAD] = part_q.astype(BF)
    kv_part[...] = dot(grad_kv[...], x[...], 0, 0)
    weighted = (part_q * wq[...].astype(F32)).astype(BF)
    ones = jnp.ones((8, HEAD), BF)
    sum_in = dot(ones, weighted, 1, 1)[0:1, :] + jnp.sum(
        kv_part[...] * kv[...].astype(F32), axis=0, keepdims=True
    )
    sums[...] = jnp.zeros((128, 128), F32)
    place = 0
    for vector in (
        sum_in / gains[0:1, :], sum_attn_out[...], sum_ff_in[...], sum_ff_out[...], sum_q, sum_k
    ):
        for first in range(0, vector.shape[1], HALF):
            for begin in range(first, min(first + HALF, vector.shape[1]), 128):
                width = min(128, first + HALF - begin)
                sums[place : place + 1, :width] = vector[:, begin : begin + width]
                place += 1
    spare = sums[...].T[:, : BACK - WIDE].astype(BF)
    pair_own_ref[...] = pair_ref[pl.ds(pl.multiple_of(row * HALF, 64), HALF), :]
    pair_sent_ref[...] = pair_ref[pl.ds(pl.multiple_of((1 - row) * HALF, 64), HALF), :]

    @pl.when(row == 0)
    def _():
        part_a[...] = kv_part[:, :HALF].astype(BF)
        part_b[...] = kv_part[:, HALF:].astype(BF)

    @pl.when(row == 1)
    def _():
        part_a[...] = kv_part[:, HALF:].astype(BF)
        part_b[...] = kv_part[:, :HALF].astype(BF)

    for j in range(8):
        held = part_a if j < 4 else part_b
        target = sent_ref if j % 4 < 2 else kept_ref
        first = (j // 4) * 2 * OWN + (j % 2) * OWN
        at = pl.multiple_of(ids[4 + j] * 64, 64)
        target[first : first + 64, D:WIDE] = held[pl.ds(at, 64), :]
        target[first + 64 : first + 128, D:WIDE] = held[pl.ds(at + HEAD, 64), :]
        target[first : first + OWN, WIDE:] = spare


def end_kernel(
    ids, near, far2, far1, far3, residual, grad_hidden, gains,
    own_ref, sent_ref, kv_ref, turned,
):
    total = summed(near, (far2, far1, far3))
    kv_ref[...] = total[:, D:].astype(BF)
    values = residual[...]
    back = norm_back(values, inverse_of(values), gains[0:1, :], total[:, :D])
    turned[...] = (grad_hidden[...] + back).T
    split_halves(ids[0], turned, own_ref, sent_ref)


def join_strips_kernel(ids, own, one, two, three, out_ref):
    join_strips(ids[3], own, one, two, three, out_ref)


def join_strips(at, own, one, two, three, out_ref):
    for step, piece in ((0, own), (1, one), (2, two), (3, three)):
        j = (at + 4 - step) % 4
        out_ref[:, pl.ds(pl.multiple_of(j * STRIDE, 128), STRIDE)] = piece[:, :STRIDE]

        @pl.when(j == 3)
        def _():
            out_ref[:, 4 * STRIDE : THREE] = piece[:, STRIDE:PIECE]


def widen_kernel(at, own, one, two, three, out_ref):
    join_strips(at[0], own, one, two, three, out_ref)
    terms = [piece[:, PIECE:].astype(F32) for piece in (own, one, two, three)]
    out_ref[:, THREE:] = ((terms[0] + terms[2]) + (terms[1] + terms[3])).astype(BF)


def results_kernel(
    ids, o0, o1, o3, o_low, o_high, p0, p1, p3, p_low, p_high,
    gate_ref, up_ref, down_ref, query_ref, out_ref, key_ref, value_ref, sums_ref, across, kv,
):
    half = LOAD // 2
    for low, high, first in ((o_low, o_high, True), (p_low, p_high, False)):
        across[:, :half] = low[...]
        across[:, half:] = high[...]
        pieces = ((0, o0), (1, o1), (3, o3)) if first else ((0, p0), (1, p1), (3, p3))
        for step, piece in pieces + ((2, across),):
            place = ((ids[2] if first else ids[3]) + 4 - step) % 4
            rows = pl.ds(pl.multiple_of(place * CHUNK, 16), CHUNK)
            for row in range(2):

                @pl.when(ids[0] == row)
                def _():
                    block = row if first else 1 - row
                    width = UNITS if block == 0 else HIDDEN - UNITS
                    for m, target in enumerate((gate_ref, up_ref, down_ref)):
                        target[rows, block * UNITS : block * UNITS + width] = piece[
                            :, m * UNITS : m * UNITS + width
                        ].astype(F32)

            if first:
                out_ref[rows, :] = piece[:, THREE : THREE + HEAD].astype(F32)

                @pl.when(place == 0)
                def _():
                    sums = piece[:64, THREE + HEAD :].astype(F32)
                    for v in range(4):
                        sums_ref[8 * v : 8 * v + 5, :] = jnp.where(
                            ids[0] == 0, sums[10 * v : 10 * v + 5], sums[10 * v + 5 : 10 * v + 10]
                        )
                    sums_ref[32:36, :] = sums[40:44]
            else:
                query_ref[rows, :] = piece[:, THREE : THREE + HEAD].astype(F32)
                kv[rows, :] = piece[:, THREE + HEAD :].astype(F32)
    turned = kv[...].T
    key_ref[...] = turned[:64]
    value_ref[...] = turned[64:]


def cross_kernel(ids, kept, got, near_ref, *refs):
    near_ref[...] = kept[:OWN, :].astype(F32) + got[:OWN, :].astype(F32)
    for i, target in enumerate(refs):
        rows = slice((i + 1) * OWN, (i + 2) * OWN)
        target[...] = (kept[rows, :].astype(F32) + got[rows, :].astype(F32)).astype(BF)


def gather_blocks(own, ready=None):
    far1, far3 = move_z(own, 1), move_z(own, 3)
    near = move_core(own)
    far2 = move_z(own, 2)
    held = [far2, far1, far3]
    if ready is not None:
        held, _ = lax.optimization_barrier((held, ready))
    return [own] + held, [near] + [move_core(block) for block in held]


def reduce_blocks(ids, sent, kept, steps=(2, 3, 1)):
    width = kept.shape[1]
    got = move_core(sent)
    near, *crossed = call(
        cross_kernel,
        [shape(OWN, width, F32)] + [shape(OWN, width, BF)] * len(steps),
        ids,
        [kept, got],
    )
    return [near] + [move_z(block, step) for block, step in zip(crossed, steps)], crossed


def ring_gather(band, axis, low_width, ready=None):
    one, three = move_plane(band, axis, 1), move_plane(band, axis, 3)
    if ready is not None:
        (one, three), _ = lax.optimization_barrier(((one, three), ready))
    low = move_plane(one[:, :low_width], axis, 1)
    high = move_plane(three[:, low_width:], axis, 3)
    return [band, one, three, low, high]


def layout(lengths_row, places):
    slots = lengths_row.shape[0]
    order = jnp.arange(slots, dtype=jnp.int32)
    ends = jnp.sum(jnp.where(order[None, :] <= order[:, None], lengths_row[None, :], 0), axis=1)
    passed = places[:, None] >= ends[None, :]
    sequence = jnp.sum(passed.astype(jnp.int32), axis=1)
    start_of = jnp.max(jnp.where(passed, ends[None, :], 0), axis=1)
    return (sequence, places - start_of, (places < ends[slots - 1]).astype(F32))


def body(
    tokens, doc_lengths, w_query, w_key, w_value, w_out, w_gate, w_up, w_down,
    gain_attn_in, gain_attn_out, gain_ff_in, gain_ff_out, gain_query, gain_key, cotangent,
):
    row = lax.axis_index("row")
    col = lax.axis_index("col")
    plane = lax.axis_index("dp")
    x_at, y_at = plane // 4, plane % 4
    near_pair, far_pair = col ^ (2 * (1 - row)), col ^ (2 * row)
    owner_cols = [col ^ 1, col ^ 3, col, col ^ 2, near_pair ^ 1, far_pair ^ 1, near_pair, far_pair]
    ids = jnp.stack([row, col, x_at, y_at] + owner_cols).astype(jnp.int32)

    def exchange_rows(block):
        turned = block.T
        own = lax.dynamic_slice_in_dim(turned, row * OWN, OWN, 1)
        return own, move_row(lax.dynamic_slice_in_dim(turned, (1 - row) * OWN, OWN, 1))

    def join_rows(own, got):
        got = got.astype(own.dtype)
        return jnp.where(
            row == 0, jnp.concatenate([own, got], axis=1), jnp.concatenate([got, own], axis=1)
        ).T

    tokens_own, tokens_other = exchange_rows(tokens)
    starts = jnp.stack(
        [
            owner_cols[j] * 256 + (row if j < 4 else 1 - row) * OWN
            for j in range(8)
        ]
    )
    places = (starts[:, None] + jnp.arange(OWN, dtype=jnp.int32)[None, :]).reshape(-1)
    sequence, positions, live = layout(doc_lengths[0], places)
    live_own = live[HEAD : HEAD + OWN][:, None]
    frequency = ROPE_BASE ** (-2.0 * jnp.arange(HEAD // 2, dtype=F32) / HEAD)
    angles = positions.astype(F32)[:, None] * frequency
    cosine, sine = jnp.cos(angles), jnp.sin(angles)
    gain_q, gain_k = gain_query[None], gain_key[None]

    gain_flat = jnp.concatenate([gain_attn_in, gain_attn_out, gain_ff_in, gain_ff_out])
    gain_own, gain_other = gain_flat.reshape(4, HALF), move_row(gain_flat).reshape(4, HALF)
    gains = jnp.where(
        row == 0,
        jnp.concatenate([gain_own, gain_other], axis=1),
        jnp.concatenate([gain_other, gain_own], axis=1),
    )

    down_turned = w_down.T
    (piece,) = call(
        piece_kernel,
        [shape(CHUNK, PIECE, BF)],
        ids,
        [w_gate, w_up, down_turned],
        [
            pltpu.VMEM((3, CHUNK, HIDDEN), BF), pltpu.VMEM((CHUNK, THREE), BF),
            pltpu.SemaphoreType.DMA((3,)),
        ],
        limit=24,
        after=(tokens_other,),
        raw=True,
        us=2,
    )
    query_other = move_row(w_query)
    kv_own = jnp.concatenate([w_key.T, w_value.T], axis=0)
    residual, payload = call(
        begin_kernel,
        [shape(OWN, D, F32), shape(OWN, WIDE, BF)],
        ids,
        [tokens_own, tokens_other, gains, kv_own],
        after=(query_other, piece, cosine),
        us=2,
    )
    mine, swapped = gather_blocks(payload)
    out_own, _ = lax.optimization_barrier((w_out.T, mine[1]))
    out_other = move_row(out_own)

    (
        normed_in, query_weights, kv_weights, pre_query, queries, pre_key, keys, values, shares,
        attended,
    ) = call(
        attention_kernel,
        [
            shape(KEYS, D, BF), shape(D, HEAD, BF), shape(2 * HEAD, D, BF),
            shape(QROWS, HEAD, F32), shape(QROWS, HEAD, BF), shape(KEYS, HEAD, BF),
            shape(KEYS, HEAD, BF), shape(KEYS, HEAD, BF), shape(QROWS, KEYS, BF),
            shape(QROWS, HEAD, BF),
        ],
        ids,
        [
            swapped[0], swapped[1], mine[0], mine[1], swapped[2], swapped[3], mine[2], mine[3],
            w_query, query_other, gain_q, gain_k, cosine, sine,
            sequence[:QROWS, None], positions[:QROWS, None], sequence[None], positions[None],
        ],
        [pltpu.VMEM((2 * HEAD, HALF), BF)] * 2,
        limit=24,
        us=10,
    )
    cot_own, cot_other = exchange_rows(cotangent)
    out_weights, sent, kept = call(
        out_kernel,
        [shape(D, HEAD, BF), shape(HEAD, D, BF), shape(HEAD, D, F32)],
        ids,
        [attended, out_own, out_other],
        us=2,
    )
    reduced, _ = reduce_blocks(ids, sent, kept, (2,))
    branch_attn, hidden_mid, normed_ff = call(
        middle_kernel,
        [shape(OWN, D, F32), shape(OWN, D, F32), shape(OWN, D, BF)],
        ids,
        reduced + [residual, gains],
    )

    moved, _ = lax.optimization_barrier((move_row(piece), attended))
    strips = [moved] + [move_plane(moved, "y", step) for step in (1, 2, 3)]
    (band,) = call(join_strips_kernel, [shape(CHUNK, THREE, BF)], ids, strips)
    weight_bands = ring_gather(band, "x", LOW, normed_ff)
    ff_weights = call(
        weights_kernel, [shape(D, UNITS, BF)] * 3, ids,
        [w_gate, w_up, down_turned] + weight_bands,
        [pltpu.VMEM((CHUNK, THREE), BF)],
        limit=24,
        us=4,
    )
    mine, swapped = gather_blocks(normed_ff, ff_weights[0])
    ff_in, activated, by_up, by_gate, sent, kept = call(
        forward_kernel,
        [shape(KEYS, D, BF)]
        + [shape(KEYS, UNITS, BF)] * 3
        + [shape(512, D, BF)] * 2,
        ids,
        swapped + mine + list(ff_weights),
        limit=24,
        us=14,
    )
    mixed_own, mixed_sent, grad_branch_ff, grad_result, sum_ff_out = call(
        turn_kernel,
        [
            shape(HALF, OWN, BF), shape(HALF, OWN, BF), shape(OWN, D, BF),
            shape(OWN, D, F32), shape(1, D, F32),
        ],
        ids,
        reduce_blocks(ids, sent, kept)[0] + [hidden_mid, cot_own, cot_other, live_own, gains],
        [pltpu.VMEM((D, OWN), F32)],
        us=3,
    )
    mine, swapped = gather_blocks(grad_branch_ff)
    ff_grad, grad_gate, grad_up, sent, kept = call(
        backward_kernel,
        [shape(KEYS, D, BF)] + [shape(KEYS, UNITS, BF)] * 2 + [shape(512, D, BF)] * 2,
        ids,
        swapped + mine + [by_up, by_gate] + list(ff_weights),
        limit=24,
        us=10,
    )
    reduced, crossed = reduce_blocks(ids, sent, kept)
    bands = call(
        products_kernel,
        (
            [shape(CHUNK, THREE, BF)] * 3
            + [shape(CHUNK, LOW, BF), shape(CHUNK, THREE - LOW, BF)]
        )
        * 2,
        ids,
        [ff_in, ff_grad, activated, grad_gate, grad_up],
        [pltpu.VMEM((D, THREE), BF)],
        limit=24,
        us=9,
        after=(crossed[0],),
    )
    grad_hidden, grad_branch_attn, sum_ff_in, sum_attn_out = call(
        return_kernel,
        [shape(OWN, D, F32), shape(OWN, D, BF), shape(1, D, F32), shape(1, D, F32)],
        ids,
        reduced + [hidden_mid, branch_attn, grad_result, gains],
        after=(bands[0],),
    )
    far = move_z(grad_branch_attn, 2)
    near, far_near = move_core(grad_branch_attn), move_core(far)
    def begin_ring(pieces, axis):
        band0, band1, band3, low, high = pieces
        one, three = call(
            join_kernel,
            [shape(CHUNK, THREE, BF)] * 2,
            ids,
            [band1, band3, move_plane(low, axis, 1), move_plane(high, axis, 3)],
        )
        return band0, move_plane(one, axis, 1), move_plane(three, axis, 3)

    own_ring, other_ring = begin_ring(bands[:5], "x"), begin_ring(bands[5:], "y")
    pair_kept, pair_sent, sent, kept = call(
        attention_back_kernel,
        [
            shape(HALF, 2 * HEAD, BF), shape(HALF, 2 * HEAD, BF), shape(512, BACK, BF),
            shape(512, BACK, BF),
        ],
        ids,
        [near, far_near, grad_branch_attn, far]
        + [
            a
            for a in (
                normed_in, query_weights, out_weights, kv_weights, pre_query, queries, pre_key, keys, values,
                shares, attended,
            )
        ]
        + [
            gain_q, gain_k, cosine, sine, gains, sum_attn_out, sum_ff_in, sum_ff_out,
        ],
        [
            pltpu.VMEM((QROWS, D), BF), pltpu.VMEM((KEYS, 2 * HEAD), BF),
            pltpu.VMEM((2 * HEAD, D), F32), pltpu.VMEM((2 * HEAD, HALF), BF),
            pltpu.VMEM((2 * HEAD, HALF), BF), pltpu.VMEM((D, 2 * HEAD), BF),
            pltpu.VMEM((128, 128), F32),
        ],
        limit=24,
        us=9,
        after=(own_ring[1], own_ring[2], other_ring[1], other_ring[2]),
    )
    pair_got = move_row(pair_sent)
    reduced, crossed = reduce_blocks(ids, sent, kept)
    tokens_grad_own, tokens_grad_sent, kv_sum = call(
        end_kernel,
        [shape(HALF, OWN, F32), shape(HALF, OWN, BF), shape(OWN, BACK - D, BF)],
        ids,
        reduced + [residual, grad_hidden, gains],
        [pltpu.VMEM((D, OWN), F32)],
    )
    mixed_got, tokens_got = move_row(mixed_sent), move_row(tokens_grad_sent)
    mixed = join_rows(mixed_own, mixed_got)
    grad_tokens = join_rows(tokens_grad_own, tokens_got)

    def reduce_two(ring, axis, second, first):
        band0, one, three = ring
        strips = call(
            functools.partial(fold_kernel, first),
            [shape(CHUNK, PIECE + EXTRA, BF)] * 4,
            ids,
            [
                band0, one, three, pair_kept, pair_got, kv_sum,
            ],
            [pltpu.VMEM((CHUNK, THREE), BF), pltpu.VMEM((HALF, EXTRA), BF)],
        )
        total = strips[0].astype(F32)
        for step in (1, 3, 2):
            total = total + move_plane(strips[step], second, step).astype(F32)
        return total.astype(BF)

    def gather_two(held, axis, second, second_at):
        strips = [held] + [move_plane(held, second, step) for step in (1, 2, 3)]
        (band,) = call(
            widen_kernel, [shape(CHUNK, LOAD, BF)], second_at[None], strips,
            after=(mixed_got, tokens_got),
        )
        return ring_gather(band, axis, LOAD // 2)

    own_total = reduce_two(own_ring, "x", "y", True)
    other_total = reduce_two(other_ring, "y", "x", False)
    peer_piece = move_row(other_total[:, :PIECE])
    own_held = jnp.concatenate([own_total[:, :PIECE], other_total[:, PIECE:]], axis=1)
    peer_held = jnp.concatenate([peer_piece, own_total[:, PIECE:]], axis=1)
    own_bands = gather_two(own_held, "x", "y", y_at)
    peer_bands = gather_two(peer_held, "y", "x", x_at)
    grad_w_gate, grad_w_up, grad_w_down, grad_w_query, grad_w_out, grad_key_w, grad_value_w, sums = call(
        results_kernel,
        [shape(HALF, HIDDEN, F32)] * 3
        + [shape(HALF, HEAD, F32)] * 2
        + [shape(64, HALF, F32)] * 2
        + [shape(40, 128, F32)],
        ids,
        own_bands + peer_bands,
        [pltpu.VMEM((CHUNK, LOAD), BF), pltpu.VMEM((HALF, 128), F32)],
        limit=48,
        after=(mixed, grad_tokens),
        us=7,
    )

    def gain_part(i):
        return sums[8 * i : 8 * i + 5].reshape(-1)[:HALF]

    return (
        mixed,
        grad_tokens,
        grad_w_query,
        grad_key_w.T,
        grad_value_w.T,
        grad_w_out.T,
        grad_w_gate,
        grad_w_up,
        grad_w_down.T,
        gain_part(0),
        gain_part(1),
        gain_part(2),
        gain_part(3),
        sums[32:34].reshape(-1),
        sums[34:36].reshape(-1),
    )


def solution(mesh):
    return jax.shard_map(
        body,
        mesh=mesh,
        in_specs=(
            P(("dp", "col"), "row"),
            P("dp", None),
            P("row", "col"),
            P("row", "col"),
            P("row", "col"),
            P("col", "row"),
            P("row", "col"),
            P("row", "col"),
            P("col", "row"),
            P("row"),
            P("row"),
            P("row"),
            P("row"),
            P(),
            P(),
            P(("dp", "col"), "row"),
        ),
        out_specs=(
            P(("dp", "col"), "row"),
            P(("dp", "col"), "row"),
            P("row", "col"),
            P("row", "col"),
            P("row", "col"),
            P("col", "row"),
            P("row", "col"),
            P("row", "col"),
            P("col", "row"),
            P("row"),
            P("row"),
            P("row"),
            P("row"),
            P(),
            P(),
        ),
        check_vma=False,
    )
```
